256 devices in a mesh: row: 16 (over x, y_hi, core), col: 16 (over z, y_lo).
Axes of the slice: x: 4, y: 4 (y_hi: 2, y_lo: 2; y = y_hi * 2 + y_lo), z: 8, core: 2. Of those that a mesh axis runs over, the one named last changes fastest.
Arguments:
- images: bfloat16 [32768, 1152], P(('row', 'col')), may hold values from -0.1875 to 0.1875
- texts: bfloat16 [32768, 1152], P(('row', 'col')), may hold values from -6 to 6
- head_weight: bfloat16 [1152, 1152], replicated, may hold values from -0.1875 to 0.1875
- head_bias: float32 [1152], replicated, may hold values from -3 to 3
- logit_scale: float32 [1], replicated, may hold values from 8 to 30
- logit_shift: float32 [1], replicated, may hold values from -6 to -2
- loss_scale: float32 [1], replicated, may hold values from 32768 to 65536
- clip_norm: float32 [1], replicated, may hold values from 72 to 144
Outputs:
- image_grad: float32 [32768, 1152], P(('row', 'col'))
- weight_grad: float32 [1152, 1152], replicated
- bias_grad: float32 [1152], replicated
- loss: float32 [1], replicated
The draws below stay inside these ranges and needn't reach their ends.
All inputs are finite; a program needn't handle non-finite values.
Results may differ from the reference program's by a relative error of at most 0.0054.
Values may be sent and summed in bfloat16 or wider, within the bound.
No kernel may reach another device: no remote copies, remote signals or barrier semaphores. Data moves between devices by JAX's collectives and lax.ppermute only.
A program may use at most 64 MiB of HBM per device.

```python
import math
import jax
import jax.numpy as jnp
from jax import lax

D = 1152
B_DEV = 128
BATCH = 32768
N_ROW = 16
N_COL = 16


def levels(rng, dims, pieces, low, largest):
    gain = 1.0
    for dim, shards_of in pieces:
        draws = jax.random.uniform(jax.random.fold_in(jax.random.fold_in(rng, 6), dim), (shards_of,), jnp.float32, low / len(pieces), largest / len(pieces))
        gain = gain * jnp.repeat(jnp.exp(draws), dims[dim] // shards_of).reshape((-1,) + (1,) * (len(dims) - 1 - dim))
    return gain


def scatter_about(stream_key, shape, scale, most, shards=(), kind=jnp.bfloat16):
    values = scale * jax.random.normal(stream_key, shape, jnp.float32)
    if shards:
        values = values * levels(stream_key, shape, shards, -0.22, 0.18)
    return jnp.clip(values, -most, most).astype(kind)


def setup_inputs(seed: int = 0) -> dict:
    keys = jax.random.split(jax.random.key(seed), 9)
    images = scatter_about(keys[0], (BATCH, D), (D ** -0.5), 0.1875, ((0, 256),))
    texts = scatter_about(keys[1], (BATCH, D), 1.0, 6.0, ((0, 256),))
    head_weight = scatter_about(keys[2], (D, D), D ** -0.5, 0.1875)
    head_bias = scatter_about(keys[3], (D,), 0.5, 3.0, (), jnp.float32)
    logit_scale = jnp.clip(jnp.exp(jax.random.uniform(keys[4], (1,), jnp.float32, math.log(8.0), math.log(30.0))), 8.0, 30.0)
    logit_shift = jnp.clip(jax.random.uniform(keys[5], (1,), jnp.float32, -6.0, -2.0), -6.0, -2.0)
    loss_scale = jnp.clip(jnp.exp(jax.random.uniform(keys[6], (1,), jnp.float32, math.log(32768.0), math.log(65536.0))), 32768.0, 65536.0)
    clip_norm = jnp.clip(jax.random.uniform(keys[7], (1,), jnp.float32, 72.0, 144.0), 72.0, 144.0)
    return {"images": images, "texts": texts, "head_weight": head_weight, "head_bias": head_bias, "logit_scale": logit_scale, "logit_shift": logit_shift, "loss_scale": loss_scale, "clip_norm": clip_norm}


EPS = 1e-06

def to_groups(values):
    width = values.shape[1]
    return jnp.transpose(jnp.reshape(values, (N_ROW, N_COL, B_DEV, width)), (1, 0, 2, 3)).reshape(N_COL, N_ROW * B_DEV, width)

def from_groups(values):
    width = values.shape[2]
    return jnp.transpose(jnp.reshape(values, (N_COL, N_ROW, B_DEV, width)), (1, 0, 2, 3)).reshape(N_ROW * N_COL * B_DEV, width)

def reference(images, texts, head_weight, head_bias, logit_scale, logit_shift, loss_scale, clip_norm):
    count = images.shape[0]
    image_full = images.astype(jnp.float32)
    inv_image = lax.rsqrt(lax.optimization_barrier(jnp.sum(image_full * image_full, axis=1, keepdims=True)) + EPS)
    x_full = image_full * inv_image
    x_b = x_full.astype(jnp.bfloat16)
    projected = jnp.dot(texts, head_weight, preferred_element_type=jnp.float32) + head_bias
    inv_text = lax.rsqrt(lax.optimization_barrier(jnp.sum(projected * projected, axis=1, keepdims=True)) + EPS)
    y_full = projected * inv_text
    y_b = y_full.astype(jnp.bfloat16)
    scale = logit_scale[0]
    shift_value = logit_shift[0]
    factor_loss = -loss_scale[0] / count

    def one_group(pair):
        x_group, y_group = pair
        logits = scale * jnp.dot(x_group, y_group.T, preferred_element_type=jnp.float32) + shift_value
        index = jnp.arange(x_group.shape[0], dtype=jnp.int32)
        signs = jnp.where(index[:, None] == index[None, :], jnp.float32(1.0), jnp.float32(-1.0))
        loss_part = jnp.sum(jax.nn.softplus(-signs * logits))
        grads = (factor_loss * signs * jax.nn.sigmoid(-signs * logits)).astype(jnp.bfloat16)
        image_part = jnp.dot(grads, y_group, preferred_element_type=jnp.float32)
        text_part = jnp.dot(grads.T, x_group, preferred_element_type=jnp.float32)
        return (loss_part, image_part, text_part)
    loss_parts, image_parts, text_parts = lax.map(one_group, (to_groups(x_b), to_groups(y_b)))
    loss = jnp.sum(loss_parts) / count
    image_side = scale * from_groups(image_parts)
    text_side = scale * from_groups(text_parts)
    image_grad = (image_side - x_full * lax.optimization_barrier(jnp.sum(x_full * image_side, axis=1, keepdims=True))) * inv_image
    text_back = (text_side - y_full * lax.optimization_barrier(jnp.sum(y_full * text_side, axis=1, keepdims=True))) * inv_text
    raw_weight = jnp.dot(texts.T, text_back.astype(jnp.bfloat16), preferred_element_type=jnp.float32)
    raw_bias = lax.optimization_barrier(jnp.sum(text_back, axis=0))
    total_norm = jnp.sqrt(jnp.sum(raw_weight * raw_weight) + jnp.sum(raw_bias * raw_bias))
    factor = jnp.minimum(jnp.float32(1.0), clip_norm[0] / total_norm)
    return (image_grad, raw_weight * factor, raw_bias * factor, jnp.reshape(loss, (1,)))
```

```python
import jax
import jax.numpy as jnp
from jax import lax
from jax.sharding import Mesh, PartitionSpec as P

EPS = 1e-06
ALL = ("x", "yh", "core", "z", "yl")
NX, NYH, NC, NZ, NYL = 4, 2, 2, 8, 2
F32, BF16 = jnp.float32, jnp.bfloat16


def place(x, yh, core, z, yl):
    return (((x * NYH + yh) * NC + core) * NZ + z) * NYL + yl


def groups_first():
    out = []
    for z in range(NZ):
        for yh in range(NYH):
            for yl in range(NYL):
                out.append([place(x, yh, 0, z, yl) for x in range(NX)])
        for x in range(NX):
            out.append([place(x, yh, 1, z, yl) for yh in range(NYH) for yl in range(NYL)])
    return out


def groups_second():
    out = []
    for x in range(NX):
        out.append([place(x, yh, 0, z, yl) for yh in range(NYH) for z in range(NZ) for yl in range(NYL)])
    for yh in range(NYH):
        for yl in range(NYL):
            out.append([place(x, yh, 1, z, yl) for x in range(NX) for z in range(NZ)])
    return out


def shifted(block, axis, distance):
    size = lax.axis_size(axis)
    return lax.ppermute(block, axis, [(i, (i + distance) % size) for i in range(size)])


def split_hi_lo(value):
    hi = value.astype(BF16)
    return hi, (value - hi.astype(F32)).astype(BF16)


def local(images, texts, head_weight, head_bias, logit_scale, logit_shift, loss_scale, clip_norm):
    own, d = images.shape
    total_rows = own * 256
    core = lax.axis_index("core")
    yc = ("yh", "core")
    txt = [texts] + [shifted(texts, "core", 1), shifted(texts, "yh", 1)]
    txt.append(lax.ppermute(texts, yc, [(0, 3), (1, 2), (2, 1), (3, 0)]))
    img = [images] + [shifted(images, "x", s) for s in (2, 1, 3)]
    t = jnp.concatenate(txt, 0)
    im = jnp.concatenate(img, 0).astype(F32)

    inv_x = lax.rsqrt(jnp.sum(im * im, axis=1, keepdims=True) + EPS)
    x_full = im * inv_x
    x_b = x_full.astype(BF16)
    u = jnp.dot(t, head_weight, preferred_element_type=F32) + head_bias
    inv_u = lax.rsqrt(jnp.sum(u * u, axis=1, keepdims=True) + EPS)
    y_full = u * inv_u
    y_b = y_full.astype(BF16)
    scale = logit_scale[0]
    z = scale * lax.dot_general(x_b, y_b, (((1,), (1,)), ((), ())), preferred_element_type=F32) + logit_shift[0]
    rows = lax.broadcasted_iota(jnp.int32, z.shape, 0)
    cols = lax.broadcasted_iota(jnp.int32, z.shape, 1)
    signs = jnp.where((rows == cols) & (rows < own), F32(1.0), F32(-1.0))
    v = -signs * z
    loss_part = jnp.sum(jax.nn.softplus(v))
    g = ((-loss_scale[0] / total_rows) * signs * jax.nn.sigmoid(v)).astype(BF16)
    dx = scale * jnp.dot(g, y_b, preferred_element_type=F32)
    dy = scale * lax.dot_general(g, x_b, (((0,), (0,)), ((), ())), preferred_element_type=F32)
    ig = (dx - x_full * jnp.sum(x_full * dx, axis=1, keepdims=True)) * inv_x
    du = (dy - y_full * jnp.sum(y_full * dy, axis=1, keepdims=True)) * inv_u
    bias_part = jnp.sum(du, axis=0)
    extra = jnp.concatenate([bias_part, loss_part[None], jnp.zeros((16 * 128 - d - 1,), F32)]).reshape(16, 128)
    hi, lo = split_hi_lo(extra)
    du_b = du.astype(BF16)
    half0 = du_b[:, :640]
    half1 = jnp.concatenate(
        [du_b[:, 640:], jnp.concatenate([hi, lo, jnp.zeros((480, 128), BF16)], 0)], 1
    )
    keep = jnp.where(core == 0, half0, half1)
    give = jnp.where(core == 0, half1, half0)
    got = shifted(give, "core", 1)
    tail = keep[:32, 512:].astype(F32) + got[:32, 512:].astype(F32)
    got = got.reshape(2, 2, own, 640)[:, ::-1].reshape(4 * own, 640)
    both = keep.astype(F32) + got.astype(F32)
    t_hi, t_lo = split_hi_lo(tail[:16] + tail[16:])
    rw = lax.dot_general(t, both.astype(BF16), (((0,), (0,)), ((), ())), preferred_element_type=F32).astype(BF16)
    block = jnp.zeros((1152, 128), BF16).at[:16].set(t_hi).at[16:32].set(t_lo)
    rw = jnp.concatenate([rw[:, :512], jnp.where(core == 0, rw[:, 512:], block)], 1)
    back = [ig[:own]] + [shifted(ig[own * k: own * (k + 1)].astype(BF16), "x", -s).astype(F32) for k, s in ((1, 2), (2, 1), (3, 3))]
    image_grad = back[0] + back[1] + back[2] + back[3]

    r1 = lax.all_to_all(rw.reshape(4, 288, 640), ALL, 0, 0, axis_index_groups=groups_first(), tiled=True)
    s1 = jnp.sum(r1.astype(F32), axis=0)
    pos1 = jnp.where(core == 0, lax.axis_index("x"), lax.axis_index(("yh", "yl")))
    flag = ((core == 1) & (pos1 == 0)).astype(F32)
    e_hi, e_lo = split_hi_lo((s1[:16, 512:] + s1[16:32, 512:]) * flag)
    tiles = s1.astype(BF16).reshape(18, 16, 5, 128).transpose(0, 2, 1, 3).reshape(1440, 128)
    zero16 = jnp.zeros((16, 128), BF16)
    tiles = jnp.concatenate([tiles, zero16, zero16, zero16, e_hi, e_lo, zero16], 0).reshape(32, 48, 128)
    r2 = lax.all_to_all(tiles, ALL, 0, 0, axis_index_groups=groups_second(), tiled=True)
    s2 = jnp.sum(r2.astype(F32), axis=0)
    pos2 = jnp.where(core == 0, lax.axis_index(("yh", "z", "yl")), lax.axis_index(("x", "z")))
    f_hi, f_lo = split_hi_lo(s2[:16] + s2[16:32])
    special = jnp.concatenate([f_hi, f_lo, zero16], 0)
    mine = jnp.where(pos2 == 31, special, s2.astype(BF16))
    a1 = lax.all_to_all(jnp.broadcast_to(mine, (32, 48, 128)), ALL, 0, 0, axis_index_groups=groups_second(), tiled=True)
    a2 = lax.all_to_all(jnp.broadcast_to(a1.reshape(1, 1536, 128), (4, 1536, 128)), ALL, 0, 0, axis_index_groups=groups_first(), tiled=True)
    other = shifted(a2, "core", 1)
    h0 = jnp.where(core == 0, a2, other)
    h1 = jnp.where(core == 0, other, a2)
    e = h1[0, 93 * 16:94 * 16].astype(F32) + h1[0, 94 * 16:95 * 16].astype(F32)
    ev = e.reshape(-1)
    raw_bias, loss_total = ev[:d], ev[d]

    def unpack(h):
        return h[:, :1440].reshape(4, 18, 5, 16, 128).transpose(0, 1, 3, 2, 4).reshape(1152, 640)

    raw_weight = jnp.concatenate([unpack(h0), unpack(h1)[:, :512]], 1).astype(F32)
    norm = jnp.sqrt(jnp.sum(raw_weight * raw_weight) + jnp.sum(raw_bias * raw_bias))
    factor = jnp.minimum(F32(1.0), clip_norm[0] / norm)
    return (image_grad, raw_weight * factor, raw_bias * factor, (loss_total / total_rows)[None])


def solution(mesh):
    fine = Mesh(mesh.devices.reshape(NX, NYH, NC, NZ, NYL), ALL)
    placed = (P(ALL, None), P(ALL, None), P(), P(), P(), P(), P(), P())
    return jax.shard_map(
        local, mesh=fine, in_specs=placed, out_specs=(P(ALL, None), P(), P(), P()), check_vma=False
    )
```

```python
import jax
import jax.numpy as jnp
from jax import lax
from jax.experimental import pallas as pl
from jax.experimental.pallas import tpu as pltpu
from jax.sharding import Mesh, PartitionSpec as P

EPS = 1e-06
ALL = ("x", "yh", "core", "z", "yl")
NX, NYH, NC, NZ, NYL = 4, 2, 2, 8, 2
F32, BF16 = jnp.float32, jnp.bfloat16
D, OWN = 1152, 128
WIDE = 640
PART = 288
TILES = 96
ONE = 16
TOTAL = 32768
BIG = pltpu.CompilerParams(vmem_limit_bytes=48 * 2**20)
VMEM = pl.BlockSpec(memory_space=pltpu.VMEM)
SMEM = pl.BlockSpec(memory_space=pltpu.SMEM)


def place(x, yh, core, z, yl):
    return (((x * NYH + yh) * NC + core) * NZ + z) * NYL + yl


def every():
    return [
        (x, yh, core, z, yl)
        for x in range(NX) for yh in range(NYH) for core in range(NC) for z in range(NZ) for yl in range(NYL)
    ]


def groups_second():
    out = []
    for x in range(NX):
        out.append([place(x, yh, 0, z, yl) for yh in range(NYH) for z in range(NZ) for yl in range(NYL)])
    for yh in range(NYH):
        for yl in range(NYL):
            out.append([place(x, yh, 1, z, yl) for x in range(NX) for z in range(NZ)])
    return out


def around(distance):
    route = []
    for x, yh, core, z, yl in every():
        if core == 0:
            to = place((x + distance) % NX, yh, core, z, yl)
        else:
            y = (2 * yh + yl + distance) % 4
            to = place(x, y // 2, core, z, y % 2)
        route.append((place(x, yh, core, z, yl), to))
    return route


def shifted(block, axis, distance):
    size = lax.axis_size(axis)
    return lax.ppermute(block, axis, [(i, (i + distance) % size) for i in range(size)])


def hi_lo(value):
    hi = value.astype(BF16)
    return hi, (value - hi.astype(F32)).astype(BF16)


def text_kernel(t0, t1, t2, t3, w_ref, b_ref, y_ref, inv_ref):
    for k, ref in enumerate((t0, t1, t2, t3)):
        rows = slice(k * OWN, (k + 1) * OWN)
        u = jnp.dot(ref[...], w_ref[...], preferred_element_type=F32) + b_ref[...]
        inv = lax.rsqrt(jnp.sum(u * u, axis=1, keepdims=True) + EPS)
        y_ref[rows, :] = u * inv
        inv_ref[rows, :] = jnp.broadcast_to(inv, (OWN, 128))


def pair_kernel(core_ref, scal_ref, i0, i1, i2, i3, y_ref, invu_ref,
                g0, g1, g2, g3, keep_ref, give_ref, xb, yb, gs, invx, ext):
    scale, shift, gfac = scal_ref[0], scal_ref[1], scal_ref[2]
    images = (i0, i1, i2, i3)
    for k, ref in enumerate(images):
        rows = slice(k * OWN, (k + 1) * OWN)
        full = ref[...].astype(F32)
        inv = lax.rsqrt(jnp.sum(full * full, axis=1, keepdims=True) + EPS)
        invx[rows, :] = jnp.broadcast_to(inv, (OWN, 128))
        xb[rows, :] = (full * inv).astype(BF16)
        yb[rows, :] = y_ref[rows, :].astype(BF16)
    loss = jnp.zeros((1, 1), F32)
    for h in range(2):
        rows = slice(h * 256, (h + 1) * 256)
        z = scale * lax.dot_general(
            xb[rows, :], yb[...], (((1,), (1,)), ((), ())), preferred_element_type=F32
        ) + shift
        if h == 0:
            r = lax.broadcasted_iota(jnp.int32, z.shape, 0)
            c = lax.broadcasted_iota(jnp.int32, z.shape, 1)
            same = (r == c) & (r < OWN)
            signs = jnp.where(same, F32(1.0), F32(-1.0))
            v = -signs * z
        else:
            signs = F32(-1.0)
            v = z
        e = jnp.exp(-jnp.abs(v))
        small = e * (1.0 - e * (0.5 - e * F32(1.0 / 3.0)))
        soft = jnp.maximum(v, 0.0) + jnp.where(e < 0.004, small, jnp.log(1.0 + e))
        loss = loss + jnp.sum(jnp.sum(soft, axis=0, keepdims=True), axis=1, keepdims=True)
        part = 1.0 / (1.0 + e)
        gs[rows, :] = (gfac * signs * jnp.where(v >= 0, part, e * part)).astype(BF16)
    for h in range(2):
        dx2 = scale * jnp.dot(gs[h * 256:(h + 1) * 256, :], yb[...], preferred_element_type=F32)
        for j in range(2):
            k = 2 * h + j
            dx = dx2[j * OWN:(j + 1) * OWN]
            inv = invx[k * OWN:(k + 1) * OWN, 0:1]
            full = images[k][...].astype(F32) * inv
            out = (dx - full * jnp.sum(full * dx, axis=1, keepdims=True)) * inv
            target = (g0, g1, g2, g3)[k]
            target[...] = out.astype(target.dtype)
    bias = jnp.zeros((1, D), F32)
    first = core_ref[0] == 0
    for h in range(2):
        rows = slice(h * 256, (h + 1) * 256)
        dy = scale * lax.dot_general(
            gs[:, rows], xb[...], (((0,), (0,)), ((), ())), preferred_element_type=F32
        )
        y = y_ref[rows, :]
        du = (dy - y * jnp.sum(y * dy, axis=1, keepdims=True)) * invu_ref[rows, 0:1]
        bias = bias + jnp.sum(du, axis=0, keepdims=True)
        left, right = du[:, :WIDE].astype(BF16), du[:, WIDE:].astype(BF16)

        @pl.when(first)
        def _():
            keep_ref[rows, :] = left
            give_ref[rows, :D - WIDE] = right

        @pl.when(jnp.logical_not(first))
        def _():
            give_ref[rows, :] = left
            keep_ref[rows, :D - WIDE] = right
    ext[...] = jnp.zeros((ONE, 128), F32)
    for r in range(D // 128):
        ext[r:r + 1, :] = bias[:, r * 128:(r + 1) * 128]
    lane = lax.broadcasted_iota(jnp.int32, (1, 128), 1)
    ext[D // 128:D // 128 + 1, :] = jnp.where(lane == 0, loss, 0.0)
    hi, lo = hi_lo(ext[...])
    rest = jnp.zeros((4 * OWN - 2 * ONE, WIDE - (D - WIDE)), BF16)

    def extras(ref):
        ref[0:ONE, D - WIDE:] = hi
        ref[ONE:2 * ONE, D - WIDE:] = lo
        ref[2 * ONE:, D - WIDE:] = rest

    @pl.when(first)
    def _():
        extras(give_ref)

    @pl.when(jnp.logical_not(first))
    def _():
        extras(keep_ref)


def head_kernel(idx_ref, t0, t1, t2, t3, keep_ref, got_ref, o0, o1, o2, o3, t_all, both, rw):
    for k, ref in enumerate((t0, t1, t2, t3)):
        rows, swap = slice(k * OWN, (k + 1) * OWN), slice((k ^ 1) * OWN, ((k ^ 1) + 1) * OWN)
        t_all[rows, :] = ref[...]
        both[rows, :] = (keep_ref[rows, :].astype(F32) + got_ref[swap, :].astype(F32)).astype(BF16)
    tail = slice(D - WIDE, WIDE)
    last = idx_ref[0] == 1
    e = keep_ref[0:2 * ONE, tail].astype(F32) + got_ref[0:2 * ONE, tail].astype(F32)
    hi, lo = hi_lo(e[:ONE] + e[ONE:])
    for q in range(4):
        rw[q] = lax.dot_general(
            t_all[:, q * PART:(q + 1) * PART], both[...], (((0,), (0,)), ((), ())), preferred_element_type=F32
        ).astype(BF16)

    @pl.when(last)
    def _():
        for q in range(4):
            rw[q, :, tail] = jnp.zeros((PART, 128), BF16)
        rw[0, 0:ONE, tail] = hi
        rw[0, ONE:2 * ONE, tail] = lo

    for s, ref in enumerate((o0, o1, o2, o3)):
        ref[...] = rw[lax.rem(idx_ref[1] + s, 4)]


def tile_kernel(idx_ref, a0, a1, a2, a3, out):
    total = a0[...].astype(F32) + a1[...].astype(F32) + a2[...].astype(F32) + a3[...].astype(F32)
    for t in range(PART // ONE):
        for l in range(WIDE // 128):
            n = t * (WIDE // 128) + l
            out[n * ONE:(n + 1) * ONE, :] = total[t * ONE:(t + 1) * ONE, l * 128:(l + 1) * 128].astype(BF16)
    out[90 * ONE:, :] = jnp.zeros((6 * ONE, 128), BF16)

    @pl.when((idx_ref[0] == 1) & (idx_ref[1] == 0))
    def _():
        hi, lo = hi_lo(total[:ONE, D - WIDE:] + total[ONE:2 * ONE, D - WIDE:])
        out[93 * ONE:94 * ONE, :] = hi
        out[94 * ONE:95 * ONE, :] = lo


def last_kernel(idx_ref, clip_ref, p0, p1, p2, p3, q0, q1, q2, q3, w_ref, b_ref, loss_ref):
    mine, theirs = (p0, p1, p2, p3), (q0, q1, q2, q3)

    def whole(left, right, at_left, at_right):
        extra = jnp.zeros((ONE, 128), F32)
        for s, ref in enumerate(right):
            here = (lax.rem(at_right + 4 - s, 4) == 0).astype(F32)
            pair = ref[93 * ONE:95 * ONE, :].astype(F32)
            extra = extra + here * (pair[:ONE] + pair[ONE:])
        bias = extra[:D // 128]
        total = jnp.zeros((ONE, 128), F32)
        for refs, lanes in ((left, 5), (right, 4)):
            for ref in refs:
                def add(t, acc, ref=ref, lanes=lanes):
                    for l in range(lanes):
                        v = ref[pl.ds(pl.multiple_of(t * 80, 16) + l * ONE, ONE), :].astype(F32)
                        acc = acc + v * v
                    return acc
                total = lax.fori_loop(0, PART // ONE, add, total)
        square = jnp.sum(total, keepdims=True) + jnp.sum(bias * bias, keepdims=True)
        factor = jnp.minimum(F32(1.0), clip_ref[0] / jnp.sqrt(square))
        for refs, lanes, base, at in ((left, 5, 0, at_left), (right, 4, WIDE, at_right)):
            for s, ref in enumerate(refs):
                row0 = lax.rem(at + 4 - s, 4) * PART

                def put(t, carry, ref=ref, lanes=lanes, base=base, row0=row0):
                    for l in range(lanes):
                        v = ref[pl.ds(pl.multiple_of(t * 80, 16) + l * ONE, ONE), :].astype(F32)
                        rows = pl.ds(pl.multiple_of(row0 + t * ONE, ONE), ONE)
                        w_ref[rows, base + l * 128:base + (l + 1) * 128] = v * factor
                    return carry
                lax.fori_loop(0, PART // ONE, put, 0)
        for r in range(D // 128):
            b_ref[0:1, r * 128:(r + 1) * 128] = bias[r:r + 1] * factor
        loss_ref[...] = extra[D // 128:D // 128 + 1, :] * F32(1.0 / TOTAL)

    @pl.when(idx_ref[0] == 0)
    def _():
        whole(mine, theirs, idx_ref[1], idx_ref[2])

    @pl.when(idx_ref[0] == 1)
    def _():
        whole(theirs, mine, idx_ref[2], idx_ref[1])


def sds(shape, kind):
    return jax.ShapeDtypeStruct(shape, kind)


def local(images, texts, head_weight, head_bias, logit_scale, logit_shift, loss_scale, clip_norm):
    core = lax.axis_index("core")
    at_x, at_y = lax.axis_index("x"), lax.axis_index(("yh", "yl"))
    at = jnp.where(core == 0, at_x, at_y)
    at_other = jnp.where(core == 0, at_y, at_x)
    idx = jnp.stack([core, at, at_other]).astype(jnp.int32)
    scal = jnp.stack([logit_scale[0], logit_shift[0], -loss_scale[0] / TOTAL])

    txt = [texts, shifted(texts, "core", 1), shifted(texts, "yh", 1)]
    txt.append(lax.ppermute(texts, ("yh", "core"), [(0, 3), (1, 2), (2, 1), (3, 0)]))
    img = [images] + [shifted(images, "x", s) for s in (2, 1, 3)]

    y_full, inv_u = pl.pallas_call(
        text_kernel,
        out_shape=(sds((4 * OWN, D), F32), sds((4 * OWN, 128), F32)),
        in_specs=[VMEM] * 6, out_specs=(VMEM, VMEM), compiler_params=BIG,
        cost_estimate=pl.CostEstimate(flops=2 * 512 * D * D, bytes_accessed=6_500_000, transcendentals=512),
        name="text_side",
    )(*txt, head_weight, head_bias[None])
    ig0, ig1, ig2, ig3, keep, give = pl.pallas_call(
        pair_kernel,
        out_shape=(sds((OWN, D), F32),) + (sds((OWN, D), BF16),) * 3 + (sds((4 * OWN, WIDE), BF16),) * 2,
        in_specs=[SMEM, SMEM] + [VMEM] * 6, out_specs=(VMEM,) * 6, compiler_params=BIG,
        scratch_shapes=[
            pltpu.VMEM((4 * OWN, D), BF16), pltpu.VMEM((4 * OWN, D), BF16), pltpu.VMEM((4 * OWN, 4 * OWN), BF16),
            pltpu.VMEM((4 * OWN, 128), F32), pltpu.VMEM((ONE, 128), F32),
        ],
        cost_estimate=pl.CostEstimate(flops=6 * 512 * 512 * D, bytes_accessed=6_500_000, transcendentals=800_000),
        name="pairs",
    )(idx, scal, *img, y_full, inv_u)

    got = shifted(give, "core", 1)
    parts = pl.pallas_call(
        head_kernel,
        out_shape=(sds((PART, WIDE), BF16),) * 4,
        in_specs=[SMEM] + [VMEM] * 6, out_specs=(VMEM,) * 4, compiler_params=BIG,
        scratch_shapes=[
            pltpu.VMEM((4 * OWN, D), BF16), pltpu.VMEM((4 * OWN, WIDE), BF16), pltpu.VMEM((4, PART, WIDE), BF16),
        ],
        cost_estimate=pl.CostEstimate(flops=2 * 512 * D * WIDE, bytes_accessed=4_000_000, transcendentals=0),
        name="head",
    )(idx, *txt, keep, got)
    r2, r1, r3 = [lax.ppermute(parts[s], ALL, around(s)) for s in (2, 1, 3)]
    tiles = pl.pallas_call(
        tile_kernel,
        out_shape=sds((TILES * ONE, 128), BF16),
        in_specs=[SMEM] + [VMEM] * 4, out_specs=VMEM, compiler_params=BIG,
        cost_estimate=pl.CostEstimate(flops=4 * PART * WIDE, bytes_accessed=1_900_000, transcendentals=0),
        name="tiles",
    )(idx, parts[0], r1, r2, r3)
    ig1, ig2, ig3, tiles = lax.optimization_barrier((ig1, ig2, ig3, tiles))
    back = [shifted(ig1, "x", -2), shifted(ig2, "x", -1), shifted(ig3, "x", -3)]
    sums = lax.all_to_all(tiles.reshape(32, 48, 128), ALL, 0, 0, axis_index_groups=groups_second(), tiled=True)
    s2 = jnp.sum(sums.astype(F32), axis=0)
    at2 = jnp.where(core == 0, lax.axis_index(("yh", "z", "yl")), lax.axis_index(("x", "z")))
    f_hi, f_lo = hi_lo(s2[:ONE] + s2[ONE:2 * ONE])
    special = jnp.concatenate([f_hi, f_lo, jnp.zeros((ONE, 128), BF16)], 0)
    mine = jnp.where(at2 == 31, special, s2.astype(BF16))
    copies = jnp.broadcast_to(mine, (32, 48, 128))
    a1 = lax.all_to_all(copies, ALL, 0, 0, axis_index_groups=groups_second(), tiled=True)
    a1, back = lax.optimization_barrier((a1, back))
    image_grad = ig0 + back[0].astype(F32) + back[1].astype(F32) + back[2].astype(F32)

    b0 = a1.reshape(TILES * ONE, 128)
    b2, b1, b3 = [lax.ppermute(b0, ALL, around(s)) for s in (2, 1, 3)]
    own_half = (b0, b1, b2, b3)
    other_half = [shifted(b, "core", 1) for b in own_half]
    weight_grad, bias_grad, loss = pl.pallas_call(
        last_kernel,
        out_shape=(sds((D, D), F32), sds((1, D), F32), sds((1, 128), F32)),
        in_specs=[SMEM, SMEM] + [VMEM] * 8, out_specs=(VMEM,) * 3, compiler_params=BIG,
        cost_estimate=pl.CostEstimate(flops=4 * D * D, bytes_accessed=8_500_000, transcendentals=0),
        name="last",
    )(idx, clip_norm, *own_half, *other_half)
    return image_grad, weight_grad, bias_grad.reshape(D), loss[0, :1]


def solution(mesh):
    fine = Mesh(mesh.devices.reshape(NX, NYH, NC, NZ, NYL), ALL)
    placed = (P(ALL, None), P(ALL, None), P(), P(), P(), P(), P(), P())
    return jax.shard_map(
        local, mesh=fine, in_specs=placed, out_specs=(P(ALL, None), P(), P(), P()), check_vma=False
    )
```

```python
import jax
import jax.numpy as jnp
from jax import lax
from jax.experimental import pallas as pl
from jax.experimental.pallas import tpu as pltpu
from jax.sharding import Mesh, PartitionSpec as P

EPS = 1e-06
ALL = ("x", "yh", "core", "z", "yl")
NX, NYH, NC, NZ, NYL = 4, 2, 2, 8, 2
F32, BF16 = jnp.float32, jnp.bfloat16
D, OWN = 1152, 128
WIDE = 640
PART = 288
TILES = 96
ONE = 16
TOTAL = 32768


def room(mib):
    return pltpu.CompilerParams(vmem_limit_bytes=mib * 2**20)


VMEM = pl.BlockSpec(memory_space=pltpu.VMEM)
SMEM = pl.BlockSpec(memory_space=pltpu.SMEM)
ANY = pl.BlockSpec(memory_space=pl.ANY)


def place(x, yh, core, z, yl):
    return (((x * NYH + yh) * NC + core) * NZ + z) * NYL + yl


def every():
    return [
        (x, yh, core, z, yl)
        for x in range(NX) for yh in range(NYH) for core in range(NC) for z in range(NZ) for yl in range(NYL)
    ]


def groups_second():
    out = []
    for x in range(NX):
        out.append([place(x, yh, 0, z, yl) for yh in range(NYH) for z in range(NZ) for yl in range(NYL)])
    for yh in range(NYH):
        for yl in range(NYL):
            out.append([place(x, yh, 1, z, yl) for x in range(NX) for z in range(NZ)])
    return out


def around(distance):
    route = []
    for x, yh, core, z, yl in every():
        if core == 0:
            to = place((x + distance) % NX, yh, core, z, yl)
        else:
            y = (2 * yh + yl + distance) % 4
            to = place(x, y // 2, core, z, y % 2)
        route.append((place(x, yh, core, z, yl), to))
    return route


def shifted(block, axis, distance):
    size = lax.axis_size(axis)
    return lax.ppermute(block, axis, [(i, (i + distance) % size) for i in range(size)])


def hi_lo(value):
    hi = value.astype(BF16)
    return hi, (value - hi.astype(F32)).astype(BF16)


def text_kernel(t_ref, w_ref, b_ref, y_ref, inv_ref):
    u = jnp.dot(t_ref[...], w_ref[...], preferred_element_type=F32) + b_ref[...]
    inv = lax.rsqrt(jnp.sum(u * u, axis=1, keepdims=True) + EPS)
    y_ref[...] = u * inv
    inv_ref[...] = jnp.broadcast_to(inv, (OWN, 128))


def pair_kernel(core_ref, scal_ref, i0, i1, i2, i3, y0, y1, y2, y3, v0, v1, v2, v3,
                gs, keep_ref, give_ref, xb, yb, ext):
    scale, shift, gfac = scal_ref[0], scal_ref[1], scal_ref[2]
    for k, ref in enumerate((i0, i1, i2, i3)):
        rows = slice(k * OWN, (k + 1) * OWN)
        full = ref[...].astype(F32)
        inv = lax.rsqrt(jnp.sum(full * full, axis=1, keepdims=True) + EPS)
        xb[rows, :] = (full * inv).astype(BF16)
        yb[rows, :] = (y0, y1, y2, y3)[k][...].astype(BF16)
    loss = jnp.zeros((1, 1), F32)
    for h in range(2):
        rows = slice(h * 256, (h + 1) * 256)
        z = scale * lax.dot_general(
            xb[rows, :], yb[...], (((1,), (1,)), ((), ())), preferred_element_type=F32
        ) + shift
        if h == 0:
            r = lax.broadcasted_iota(jnp.int32, z.shape, 0)
            c = lax.broadcasted_iota(jnp.int32, z.shape, 1)
            same = (r == c) & (r < OWN)
            signs = jnp.where(same, F32(1.0), F32(-1.0))
            v = -signs * z
        else:
            signs = F32(-1.0)
            v = z
        e = jnp.exp(-jnp.abs(v))
        small = e * (1.0 - e * (0.5 - e * F32(1.0 / 3.0)))
        soft = jnp.maximum(v, 0.0) + jnp.where(e < 0.004, small, jnp.log(1.0 + e))
        loss = loss + jnp.sum(jnp.sum(soft, axis=0, keepdims=True), axis=1, keepdims=True)
        part = 1.0 / (1.0 + e)
        gs[rows, :] = (gfac * signs * jnp.where(v >= 0, part, e * part)).astype(BF16)
    bias = jnp.zeros((1, D), F32)
    first = core_ref[0] == 0
    for h in range(2):
        rows = slice(h * 256, (h + 1) * 256)
        dy = scale * lax.dot_general(
            gs[:, rows], xb[...], (((0,), (0,)), ((), ())), preferred_element_type=F32
        )
        for j in range(2):
            k = 2 * h + j
            here = slice(k * OWN, (k + 1) * OWN)
            dyk = dy[j * OWN:(j + 1) * OWN]
            y = (y0, y1, y2, y3)[k][...]
            du = (dyk - y * jnp.sum(y * dyk, axis=1, keepdims=True)) * (v0, v1, v2, v3)[k][:, 0:1]
            bias = bias + jnp.sum(du, axis=0, keepdims=True)
            left, right = du[:, :WIDE].astype(BF16), du[:, WIDE:].astype(BF16)

            @pl.when(first)
            def _():
                keep_ref[here, :] = left
                give_ref[here, :D - WIDE] = right

            @pl.when(jnp.logical_not(first))
            def _():
                give_ref[here, :] = left
                keep_ref[here, :D - WIDE] = right
    ext[...] = jnp.zeros((ONE, 128), F32)
    for r in range(D // 128):
        ext[r:r + 1, :] = bias[:, r * 128:(r + 1) * 128]
    lane = lax.broadcasted_iota(jnp.int32, (1, 128), 1)
    ext[D // 128:D // 128 + 1, :] = jnp.where(lane == 0, loss, 0.0)
    hi, lo = hi_lo(ext[...])
    rest = jnp.zeros((4 * OWN - 2 * ONE, WIDE - (D - WIDE)), BF16)

    def extras(ref):
        ref[0:ONE, D - WIDE:] = hi
        ref[ONE:2 * ONE, D - WIDE:] = lo
        ref[2 * ONE:, D - WIDE:] = rest

    @pl.when(first)
    def _():
        extras(give_ref)

    @pl.when(jnp.logical_not(first))
    def _():
        extras(keep_ref)


def image_kernel(scal_ref, i0, i1, i2, i3, y0, y1, y2, y3, gs, g0, g1, g2, g3, yb):
    scale = scal_ref[0]
    for k, ref in enumerate((y0, y1, y2, y3)):
        yb[k * OWN:(k + 1) * OWN, :] = ref[...].astype(BF16)
    for h in range(2):
        dx2 = scale * jnp.dot(gs[h * 256:(h + 1) * 256, :], yb[...], preferred_element_type=F32)
        for j in range(2):
            k = 2 * h + j
            dx = dx2[j * OWN:(j + 1) * OWN]
            full = (i0, i1, i2, i3)[k][...].astype(F32)
            inv = lax.rsqrt(jnp.sum(full * full, axis=1, keepdims=True) + EPS)
            full = full * inv
            out = (dx - full * jnp.sum(full * dx, axis=1, keepdims=True)) * inv
            target = (g0, g1, g2, g3)[k]
            target[...] = out.astype(target.dtype)


def head_kernel(idx_ref, t0, t1, t2, t3, keep_ref, got_ref, o0, o1, o2, o3, t_all, both, rw):
    for k, ref in enumerate((t0, t1, t2, t3)):
        rows, swap = slice(k * OWN, (k + 1) * OWN), slice((k ^ 1) * OWN, ((k ^ 1) + 1) * OWN)
        t_all[rows, :] = ref[...]
        both[rows, :] = (keep_ref[rows, :].astype(F32) + got_ref[swap, :].astype(F32)).astype(BF16)
    tail = slice(D - WIDE, WIDE)
    last = idx_ref[0] == 1
    e = keep_ref[0:2 * ONE, tail].astype(F32) + got_ref[0:2 * ONE, tail].astype(F32)
    hi, lo = hi_lo(e[:ONE] + e[ONE:])
    for q in range(4):
        rw[q] = lax.dot_general(
            t_all[:, q * PART:(q + 1) * PART], both[...], (((0,), (0,)), ((), ())), preferred_element_type=F32
        ).astype(BF16)

    @pl.when(last)
    def _():
        for q in range(4):
            rw[q, :, tail] = jnp.zeros((PART, 128), BF16)
        rw[0, 0:ONE, tail] = hi
        rw[0, ONE:2 * ONE, tail] = lo

    for s, ref in enumerate((o0, o1, o2, o3)):
        ref[...] = rw[lax.rem(idx_ref[1] + s, 4)]


def tile_kernel(idx_ref, a0, a1, a2, a3, out):
    total = a0[...].astype(F32) + a1[...].astype(F32) + a2[...].astype(F32) + a3[...].astype(F32)
    for t in range(PART // ONE):
        for l in range(WIDE // 128):
            n = t * (WIDE // 128) + l
            n = 3 * (31 - n // 3) + n % 3
            out[n * ONE:(n + 1) * ONE, :] = total[t * ONE:(t + 1) * ONE, l * 128:(l + 1) * 128].astype(BF16)
    out[:6 * ONE, :] = jnp.zeros((6 * ONE, 128), BF16)

    @pl.when((idx_ref[0] == 1) & (idx_ref[1] == 0))
    def _():
        hi, lo = hi_lo(total[:ONE, D - WIDE:] + total[ONE:2 * ONE, D - WIDE:])
        out[:ONE, :] = hi
        out[ONE:2 * ONE, :] = lo


def last_kernel(idx_ref, clip_ref, p0, p1, p2, p3, q0, q1, q2, q3, w_ref, b_ref, loss_ref,
                slots, wide_slots, out_sem):
    parts = (p0, p1, p2, p3, q0, q1, q2, q3)

    def whole(left, right, at_left, at_right):
        total = jnp.zeros((ONE, 128), F32)
        extra = jnp.zeros((ONE, 128), F32)
        for s in range(4):
            for n, lanes in ((left + s, 5), (right + s, 4)):

                def add(t, acc, n=n, lanes=lanes):
                    v = parts[n][pl.ds(pl.multiple_of(t * 80, ONE), lanes * ONE), :].astype(F32)
                    v = v * v
                    here = [v[l * ONE:(l + 1) * ONE] for l in range(lanes)]
                    while len(here) > 1:
                        here = [sum(here[i:i + 2][1:], here[i]) for i in range(0, len(here), 2)]
                    return acc + here[0]
                total = lax.fori_loop(0, PART // ONE, add, total, unroll=6)
            here = (lax.rem(at_right + 4 - s, 4) == 0).astype(F32)
            pair = parts[right + s][93 * ONE:95 * ONE, :].astype(F32)
            extra = extra + here * (pair[:ONE] + pair[ONE:])
        bias = extra[:D // 128]
        square = jnp.sum(total, keepdims=True) + jnp.sum(bias * bias, keepdims=True)
        factor = jnp.minimum(F32(1.0), clip_ref[0] / jnp.sqrt(square))
        outs = []
        for s in range(4):
            for n, lanes, base, at, slot in ((left + s, 5, 0, at_left, wide_slots), (right + s, 4, WIDE, at_right, slots)):
                def put(t, carry, n=n, lanes=lanes, slot=slot, s=s):
                    v = parts[n][pl.ds(pl.multiple_of(t * 80, ONE), lanes * ONE), :].astype(F32) * factor
                    rows = pl.ds(pl.multiple_of(t * ONE, ONE), ONE)
                    for l in range(lanes):
                        slot[s, rows, l * 128:(l + 1) * 128] = v[l * ONE:(l + 1) * ONE]
                    return carry
                lax.fori_loop(0, PART // ONE, put, 0, unroll=6)
                row0 = pl.multiple_of(lax.rem(at + 4 - s, 4) * PART, PART)
                out = pltpu.make_async_copy(
                    slot.at[s], w_ref.at[pl.ds(row0, PART), base:base + lanes * 128], out_sem.at[len(outs)]
                )
                out.start()
                outs.append(out)
        for r in range(D // 128):
            b_ref[r * 128:(r + 1) * 128] = (bias[r:r + 1] * factor).reshape(128)
        loss_ref[0] = jnp.sum(extra[D // 128:D // 128 + 1, :]) * F32(1.0 / TOTAL)
        for out in outs:
            out.wait()

    @pl.when(idx_ref[0] == 0)
    def _():
        whole(0, 4, idx_ref[1], idx_ref[2])

    @pl.when(idx_ref[0] == 1)
    def _():
        whole(4, 0, idx_ref[2], idx_ref[1])


def sds(shape, kind):
    return jax.ShapeDtypeStruct(shape, kind)


def local(images, texts, head_weight, head_bias, logit_scale, logit_shift, loss_scale, clip_norm):
    core = lax.axis_index("core")
    at_x, at_y = lax.axis_index("x"), lax.axis_index(("yh", "yl"))
    at = jnp.where(core == 0, at_x, at_y)
    at_other = jnp.where(core == 0, at_y, at_x)
    idx = jnp.stack([core, at, at_other]).astype(jnp.int32)
    scal = jnp.stack([logit_scale[0], logit_shift[0], -loss_scale[0] / TOTAL])

    txt = [texts, shifted(texts, "core", 1), shifted(texts, "yh", 1)]
    txt.append(lax.ppermute(texts, ("yh", "core"), [(0, 3), (1, 2), (2, 1), (3, 0)]))
    img = [images] + [shifted(images, "x", s) for s in (2, 1, 3)]

    bias_row = head_bias[None]
    sides = [
        pl.pallas_call(
            text_kernel,
            out_shape=(sds((OWN, D), F32), sds((OWN, 128), F32)),
            in_specs=[VMEM] * 3, out_specs=(VMEM, VMEM), compiler_params=room(10),
            cost_estimate=pl.CostEstimate(flops=2 * OWN * D * D, bytes_accessed=3_600_000, transcendentals=OWN),
            name="text_side",
        )(block, head_weight, bias_row)
        for block in txt
    ]
    ys, invs = [y for y, _ in sides], [v for _, v in sides]
    gs, keep, give = pl.pallas_call(
        pair_kernel,
        out_shape=(sds((4 * OWN, 4 * OWN), BF16),) + (sds((4 * OWN, WIDE), BF16),) * 2,
        in_specs=[SMEM, SMEM] + [VMEM] * 12, out_specs=(VMEM,) * 3, compiler_params=room(20),
        scratch_shapes=[
            pltpu.VMEM((4 * OWN, D), BF16), pltpu.VMEM((4 * OWN, D), BF16), pltpu.VMEM((ONE, 128), F32),
        ],
        cost_estimate=pl.CostEstimate(flops=4 * 512 * 512 * D, bytes_accessed=5_500_000, transcendentals=800_000),
        name="pairs",
    )(idx, scal, *img, *ys, *invs)
    ig0, ig1, ig2, ig3 = pl.pallas_call(
        image_kernel,
        out_shape=(sds((OWN, D), F32),) + (sds((OWN, D), BF16),) * 3,
        in_specs=[SMEM] + [VMEM] * 9, out_specs=(VMEM,) * 4, compiler_params=room(20),
        scratch_shapes=[pltpu.VMEM((4 * OWN, D), BF16)],
        cost_estimate=pl.CostEstimate(flops=2 * 512 * 512 * D, bytes_accessed=5_500_000, transcendentals=512),
        name="image_side",
    )(scal, *img, *ys, gs)

    got = shifted(give, "core", 1)
    parts = pl.pallas_call(
        head_kernel,
        out_shape=(sds((PART, WIDE), BF16),) * 4,
        in_specs=[SMEM] + [VMEM] * 6, out_specs=(VMEM,) * 4, compiler_params=room(14),
        scratch_shapes=[
            pltpu.VMEM((4 * OWN, D), BF16), pltpu.VMEM((4 * OWN, WIDE), BF16), pltpu.VMEM((4, PART, WIDE), BF16),
        ],
        cost_estimate=pl.CostEstimate(flops=2 * 512 * D * WIDE, bytes_accessed=4_000_000, transcendentals=0),
        name="head",
    )(idx, *txt, keep, got)
    r2, r1, r3 = [lax.ppermute(parts[s], ALL, around(s)) for s in (2, 1, 3)]
    tiles = pl.pallas_call(
        tile_kernel,
        out_shape=sds((TILES * ONE, 128), BF16),
        in_specs=[SMEM] + [VMEM] * 4, out_specs=VMEM, compiler_params=room(8),
        cost_estimate=pl.CostEstimate(flops=4 * PART * WIDE, bytes_accessed=1_900_000, transcendentals=0),
        name="tiles",
    )(idx, parts[0], r1, r2, r3)
    ig1, ig2, ig3, tiles = lax.optimization_barrier((ig1, ig2, ig3, tiles))
    back = [shifted(ig1, "x", -2), shifted(ig2, "x", -1), shifted(ig3, "x", -3)]
    sums = lax.all_to_all(tiles.reshape(32, 48, 128), ALL, 0, 0, axis_index_groups=groups_second(), tiled=True)
    sums, back[1], back[2] = lax.optimization_barrier((sums, back[1], back[2]))
    s2 = jnp.sum(sums.astype(F32), axis=0)
    at2 = jnp.where(core == 0, lax.axis_index(("yh", "z", "yl")), lax.axis_index(("x", "z")))
    f_hi, f_lo = hi_lo(s2[:ONE] + s2[ONE:2 * ONE])
    special = jnp.concatenate([f_hi, f_lo, jnp.zeros((ONE, 128), BF16)], 0)
    mine = jnp.where(at2 == 0, special, s2.astype(BF16))
    copies = jnp.broadcast_to(mine, (32, 48, 128))
    turned = [group[::-1] for group in groups_second()]
    a1 = lax.all_to_all(copies, ALL, 0, 0, axis_index_groups=turned, tiled=True)
    a1, back = lax.optimization_barrier((a1, back))
    image_grad = ig0 + back[0].astype(F32) + back[1].astype(F32) + back[2].astype(F32)

    b0 = a1.reshape(TILES * ONE, 128)
    b2, b1, b3 = [lax.ppermute(b0, ALL, around(s)) for s in (2, 1, 3)]
    own_half = (b0, b1, b2, b3)
    other_half = [shifted(b, "core", 1) for b in own_half]
    weight_grad, bias_grad, loss = pl.pallas_call(
        last_kernel,
        out_shape=(sds((D, D), F32), sds((D,), F32), sds((1,), F32)),
        in_specs=[SMEM, SMEM] + [VMEM] * 8, out_specs=(ANY, VMEM, SMEM), compiler_params=room(14),
        scratch_shapes=[
            pltpu.VMEM((4, PART, D - WIDE), F32), pltpu.VMEM((4, PART, WIDE), F32), pltpu.SemaphoreType.DMA((8,)),
        ],
        cost_estimate=pl.CostEstimate(flops=4 * D * D, bytes_accessed=8_500_000, transcendentals=0),
        name="last",
    )(idx, clip_norm, *own_half, *other_half)
    return image_grad, weight_grad, bias_grad, loss


def solution(mesh):
    fine = Mesh(mesh.devices.reshape(NX, NYH, NC, NZ, NYL), ALL)
    placed = (P(ALL, None), P(ALL, None), P(), P(), P(), P(), P(), P())
    return jax.shard_map(
        local, mesh=fine, in_specs=placed, out_specs=(P(ALL, None), P(), P(), P()), check_vma=False
    )
```

```python
import jax
import jax.numpy as jnp
from jax import lax
from jax.experimental import pallas as pl
from jax.experimental.pallas import tpu as pltpu
from jax.sharding import Mesh, PartitionSpec as P

EPS = 1e-06
ALL = ("x", "yh", "core", "z", "yl")
NX, NYH, NC, NZ, NYL = 4, 2, 2, 8, 2
F32, BF16 = jnp.float32, jnp.bfloat16
D, OWN = 1152, 128
WIDE = 640
PART = 288
ONE = 16
LANES = 4
HALF = PART // 2
REAL = 81
USED = 83 * ONE
ALLOT = 96 * ONE
TOTAL = 32768


def room(mib):
    return pltpu.CompilerParams(vmem_limit_bytes=mib * 2**20)


VMEM = pl.BlockSpec(memory_space=pltpu.VMEM)
SMEM = pl.BlockSpec(memory_space=pltpu.SMEM)
ANY = pl.BlockSpec(memory_space=pl.ANY)


def place(x, yh, core, z, yl):
    return (((x * NYH + yh) * NC + core) * NZ + z) * NYL + yl


def every():
    return [
        (x, yh, core, z, yl)
        for x in range(NX) for yh in range(NYH) for core in range(NC) for z in range(NZ) for yl in range(NYL)
    ]


def groups_second():
    out = []
    for x in range(NX):
        out.append([place(x, yh, 0, z, yl) for z in range(NZ) for yh in range(NYH) for yl in range(NYL)])
    for yh in range(NYH):
        for yl in range(NYL):
            out.append([place(x, yh, 1, z, yl) for z in range(NZ) for x in range(NX)])
    return out


def around(distance):
    route = []
    for x, yh, core, z, yl in every():
        if core == 0:
            to = place((x + distance) % NX, yh, core, z, yl)
        else:
            y = (2 * yh + yl + distance) % 4
            to = place(x, y // 2, core, z, y % 2)
        route.append((place(x, yh, core, z, yl), to))
    return route


def shifted(block, axis, distance):
    size = lax.axis_size(axis)
    return lax.ppermute(block, axis, [(i, (i + distance) % size) for i in range(size)])


def hi_lo(value):
    hi = value.astype(BF16)
    return hi, (value - hi.astype(F32)).astype(BF16)


def text_kernel(t_ref, w_ref, b_ref, y_ref, inv_ref, flip_ref):
    flip_ref[...] = t_ref[...].T
    u = jnp.dot(t_ref[...], w_ref[...], preferred_element_type=F32) + b_ref[...]
    inv = lax.rsqrt(jnp.sum(u * u, axis=1, keepdims=True) + EPS)
    y_ref[...] = u * inv
    inv_ref[...] = jnp.broadcast_to(inv, (OWN, 128))


def pair_kernel(core_ref, scal_ref, i0, i1, i2, i3, y0, y1, y2, y3, v0, v1, v2, v3,
                gs, keep_ref, give_ref, xb, yb, ext):
    scale, shift, gfac = scal_ref[0], scal_ref[1], scal_ref[2]
    for k, ref in enumerate((i0, i1, i2, i3)):
        rows = slice(k * OWN, (k + 1) * OWN)
        full = ref[...].astype(F32)
        inv = lax.rsqrt(jnp.sum(full * full, axis=1, keepdims=True) + EPS)
        xb[rows, :] = (full * inv).astype(BF16)
        yb[rows, :] = (y0, y1, y2, y3)[k][...].astype(BF16)
    loss = jnp.zeros((1, 1), F32)
    for h in range(2):
        rows = slice(h * 256, (h + 1) * 256)
        z = scale * lax.dot_general(
            xb[rows, :], yb[...], (((1,), (1,)), ((), ())), preferred_element_type=F32
        ) + shift
        if h == 0:
            r = lax.broadcasted_iota(jnp.int32, z.shape, 0)
            c = lax.broadcasted_iota(jnp.int32, z.shape, 1)
            same = (r == c) & (r < OWN)
            signs = jnp.where(same, F32(1.0), F32(-1.0))
            v = -signs * z
        else:
            signs = F32(-1.0)
            v = z
        e = jnp.exp(-jnp.abs(v))
        small = e * (1.0 - e * (0.5 - e * F32(1.0 / 3.0)))
        soft = jnp.maximum(v, 0.0) + jnp.where(e < 0.004, small, jnp.log(1.0 + e))
        loss = loss + jnp.sum(jnp.sum(soft, axis=0, keepdims=True), axis=1, keepdims=True)
        part = 1.0 / (1.0 + e)
        gs[rows, :] = (gfac * signs * jnp.where(v >= 0, part, e * part)).astype(BF16)
    bias = jnp.zeros((1, D), F32)
    first = core_ref[0] == 0
    for h in range(2):
        rows = slice(h * 256, (h + 1) * 256)
        dy = scale * lax.dot_general(
            gs[:, rows], xb[...], (((0,), (0,)), ((), ())), preferred_element_type=F32
        )
        for j in range(2):
            k = 2 * h + j
            here = slice(k * OWN, (k + 1) * OWN)
            dyk = dy[j * OWN:(j + 1) * OWN]
            y = (y0, y1, y2, y3)[k][...]
            du = (dyk - y * jnp.sum(y * dyk, axis=1, keepdims=True)) * (v0, v1, v2, v3)[k][:, 0:1]
            bias = bias + jnp.sum(du, axis=0, keepdims=True)
            parts = [du[:, 512 * c:512 * (c + 1)].astype(BF16) for c in range(2)]
            shared = du[:, 1024:].astype(BF16)
            keep_ref[here, 512:] = shared
            give_ref[here, 512:] = shared

            @pl.when(first)
            def _():
                keep_ref[here, :512] = parts[0]
                give_ref[here, :512] = parts[1]

            @pl.when(jnp.logical_not(first))
            def _():
                give_ref[here, :512] = parts[0]
                keep_ref[here, :512] = parts[1]
    ext[...] = jnp.zeros((ONE, 128), F32)
    for r in range(D // 128):
        ext[r:r + 1, :] = bias[:, r * 128:(r + 1) * 128]
    lane = lax.broadcasted_iota(jnp.int32, (1, 128), 1)
    ext[D // 128:D // 128 + 1, :] = jnp.where(lane == 0, loss, 0.0)
    hi, lo = hi_lo(ext[...])
    for ref in (keep_ref, give_ref):
        ref[4 * OWN:, 128:] = jnp.zeros((2 * ONE, WIDE - 128), BF16)
        ref[4 * OWN:4 * OWN + ONE, :128] = hi
        ref[4 * OWN + ONE:, :128] = lo


def image_kernel(scal_ref, i0, i1, i2, i3, y0, y1, y2, y3, gs, g0, g1, g2, g3, yb):
    scale = scal_ref[0]
    for k, ref in enumerate((y0, y1, y2, y3)):
        yb[k * OWN:(k + 1) * OWN, :] = ref[...].astype(BF16)
    for h in range(2):
        dx2 = scale * jnp.dot(gs[h * 256:(h + 1) * 256, :], yb[...], preferred_element_type=F32)
        for j in range(2):
            k = 2 * h + j
            dx = dx2[j * OWN:(j + 1) * OWN]
            full = (i0, i1, i2, i3)[k][...].astype(F32)
            inv = lax.rsqrt(jnp.sum(full * full, axis=1, keepdims=True) + EPS)
            full = full * inv
            out = (dx - full * jnp.sum(full * dx, axis=1, keepdims=True)) * inv
            target = (g0, g1, g2, g3)[k]
            target[...] = out.astype(target.dtype)


def head_kernel(idx_ref, f0, f1, f2, f3, keep_ref, got_ref, o0, o1, o2, o3, flips, both, rw, shared):
    for k, ref in enumerate((f0, f1, f2, f3)):
        rows, swap = slice(k * OWN, (k + 1) * OWN), slice((k ^ 1) * OWN, ((k ^ 1) + 1) * OWN)
        flips[:, rows] = ref[...]
        both[rows, :] = (keep_ref[rows, :].astype(F32) + got_ref[swap, :].astype(F32)).astype(BF16)
    e = keep_ref[4 * OWN:, :128].astype(F32) + got_ref[4 * OWN:, :128].astype(F32)
    hi, lo = hi_lo(e[:ONE] + e[ONE:])
    for q in range(4):
        part = jnp.dot(flips[q * PART:(q + 1) * PART, :], both[...], preferred_element_type=F32).astype(BF16)
        for t in range(PART // ONE):
            for l in range(LANES):
                n = t * LANES + l
                rw[q, n * ONE:(n + 1) * ONE, :] = part[t * ONE:(t + 1) * ONE, l * 128:(l + 1) * 128]
        shared[q] = part[:, 512:]
        rw[q, 72 * ONE:REAL * ONE, :] = shared[q, pl.ds(pl.multiple_of(idx_ref[0] * HALF, HALF), HALF), :]
        rw[q, REAL * ONE:, :] = jnp.zeros((2 * ONE, 128), BF16)
    rw[0, REAL * ONE:(REAL + 1) * ONE, :] = hi
    rw[0, (REAL + 1) * ONE:, :] = lo
    for s, ref in enumerate((o0, o1, o2, o3)):
        ref[...] = rw[lax.rem(idx_ref[1] + s, 4)]


def tile_kernel(a0, a1, a2, a3, out):
    total = a0[...].astype(F32) + a1[...].astype(F32) + a2[...].astype(F32) + a3[...].astype(F32)
    group = 3 * ONE
    for j in range(27):
        out[(31 - j) * group:(32 - j) * group, :] = total[j * group:(j + 1) * group].astype(BF16)
    hi, lo = hi_lo(total[REAL * ONE:(REAL + 1) * ONE] + total[(REAL + 1) * ONE:])
    out[4 * group:4 * group + ONE, :] = hi
    out[4 * group + ONE:4 * group + 2 * ONE, :] = lo
    out[4 * group + 2 * ONE:5 * group, :] = jnp.zeros((ONE, 128), BF16)
    out[:4 * group, :] = jnp.zeros((4 * group, 128), BF16)


def last_kernel(idx_ref, clip_ref, p0, p1, p2, p3, q0, q1, q2, q3, w_ref, b_ref, loss_ref, slots, shared, out_sem):
    parts = (p0, p1, p2, p3, q0, q1, q2, q3)

    def whole(left, right, at_left, at_right):
        total = jnp.zeros((3 * ONE, 128), F32)
        extra = jnp.zeros((ONE, 128), F32)
        for s in range(4):
            for n in (left + s, right + s):
                def add(t, acc, n=n):
                    v = parts[n][pl.ds(pl.multiple_of(t * 3 * ONE, ONE), 3 * ONE), :].astype(F32)
                    return acc + v * v
                total = lax.fori_loop(0, REAL // 3, add, total, unroll=9)
            here = (lax.rem(at_left + 4 - s, 4) == 0).astype(F32)
            pair = parts[left + s][REAL * ONE:, :].astype(F32)
            extra = extra + here * (pair[:ONE] + pair[ONE:])
        bias = extra[:D // 128]
        square = jnp.sum(total, keepdims=True) + jnp.sum(bias * bias, keepdims=True)
        factor = jnp.minimum(F32(1.0), clip_ref[0] / jnp.sqrt(square))
        outs = []
        for s in range(4):
            for side, n, at in ((0, left + s, at_left), (1, right + s, at_right)):
                def put(t, carry, n=n, side=side, s=s):
                    v = parts[n][pl.ds(pl.multiple_of(t * LANES * ONE, ONE), LANES * ONE), :].astype(F32) * factor
                    rows = pl.ds(pl.multiple_of(t * ONE, ONE), ONE)
                    for l in range(LANES):
                        slots[side, s, rows, l * 128:(l + 1) * 128] = v[l * ONE:(l + 1) * ONE]
                    return carry
                lax.fori_loop(0, PART // ONE, put, 0, unroll=6)
                shared[side, s] = parts[n][72 * ONE:REAL * ONE, :].astype(F32) * factor
                row0 = lax.rem(at + 4 - s, 4) * PART
                whole_rows = pl.ds(pl.multiple_of(row0, PART), PART)
                half_rows = pl.ds(pl.multiple_of(row0 + side * HALF, HALF), HALF)
                for source, target in (
                    (slots.at[side, s], w_ref.at[whole_rows, side * 512:(side + 1) * 512]),
                    (shared.at[side, s], w_ref.at[half_rows, 1024:D]),
                ):
                    out = pltpu.make_async_copy(source, target, out_sem.at[len(outs)])
                    out.start()
                    outs.append(out)
        for r in range(D // 128):
            b_ref[r * 128:(r + 1) * 128] = (bias[r:r + 1] * factor).reshape(128)
        loss_ref[0] = jnp.sum(extra[D // 128:D // 128 + 1, :]) * F32(1.0 / TOTAL)
        for out in outs:
            out.wait()

    @pl.when(idx_ref[0] == 0)
    def _():
        whole(0, 4, idx_ref[1], idx_ref[2])

    @pl.when(idx_ref[0] == 1)
    def _():
        whole(4, 0, idx_ref[2], idx_ref[1])


def sds(shape, kind):
    return jax.ShapeDtypeStruct(shape, kind)


def local(images, texts, head_weight, head_bias, logit_scale, logit_shift, loss_scale, clip_norm):
    core = lax.axis_index("core")
    at_x, at_y = lax.axis_index("x"), lax.axis_index(("yh", "yl"))
    at = jnp.where(core == 0, at_x, at_y)
    at_other = jnp.where(core == 0, at_y, at_x)
    idx = jnp.stack([core, at, at_other]).astype(jnp.int32)
    scal = jnp.stack([logit_scale[0], logit_shift[0], -loss_scale[0] / TOTAL])

    cross = lax.ppermute(texts, ("yh", "core"), [(0, 3), (1, 2), (2, 1), (3, 0)])
    near, cross = lax.optimization_barrier((texts, cross))
    txt = [texts, shifted(near, "core", 1), shifted(texts, "yh", 1), cross]
    img = [images] + [shifted(images, "x", s) for s in (2, 1, 3)]

    bias_row = head_bias[None]
    sides = [
        pl.pallas_call(
            text_kernel,
            out_shape=(sds((OWN, D), F32), sds((OWN, 128), F32), sds((D, OWN), BF16)),
            in_specs=[VMEM] * 3, out_specs=(VMEM,) * 3, compiler_params=room(10),
            cost_estimate=pl.CostEstimate(flops=2 * OWN * D * D, bytes_accessed=3_600_000, transcendentals=OWN),
            name="text_side",
        )(block, head_weight, bias_row)
        for block in txt
    ]
    ys, invs, flips = zip(*sides)
    gs, keep, give = pl.pallas_call(
        pair_kernel,
        out_shape=(sds((4 * OWN, 4 * OWN), BF16),) + (sds((4 * OWN + 2 * ONE, WIDE), BF16),) * 2,
        in_specs=[SMEM, SMEM] + [VMEM] * 12, out_specs=(VMEM,) * 3, compiler_params=room(20),
        scratch_shapes=[
            pltpu.VMEM((4 * OWN, D), BF16), pltpu.VMEM((4 * OWN, D), BF16), pltpu.VMEM((ONE, 128), F32),
        ],
        cost_estimate=pl.CostEstimate(flops=4 * 512 * 512 * D, bytes_accessed=5_500_000, transcendentals=800_000),
        name="pairs",
    )(idx, scal, *img, *ys, *invs)
    ig0, ig1, ig2, ig3 = pl.pallas_call(
        image_kernel,
        out_shape=(sds((OWN, D), F32),) + (sds((OWN, D), BF16),) * 3,
        in_specs=[SMEM] + [VMEM] * 9, out_specs=(VMEM,) * 4, compiler_params=room(20),
        scratch_shapes=[pltpu.VMEM((4 * OWN, D), BF16)],
        cost_estimate=pl.CostEstimate(flops=2 * 512 * 512 * D, bytes_accessed=5_500_000, transcendentals=512),
        name="image_side",
    )(scal, *img, *ys, gs)

    got = shifted(give, "core", 1)
    parts = pl.pallas_call(
        head_kernel,
        out_shape=(sds((USED, 128), BF16),) * 4,
        in_specs=[SMEM] + [VMEM] * 6, out_specs=(VMEM,) * 4, compiler_params=room(14),
        scratch_shapes=[
            pltpu.VMEM((D, 4 * OWN), BF16), pltpu.VMEM((4 * OWN, WIDE), BF16),
            pltpu.VMEM((4, USED, 128), BF16), pltpu.VMEM((4, PART, 128), BF16),
        ],
        cost_estimate=pl.CostEstimate(flops=2 * 512 * D * WIDE, bytes_accessed=4_000_000, transcendentals=0),
        name="head",
    )(idx, *flips, keep, got)
    r2, r1, r3 = [lax.ppermute(parts[s], ALL, around(s)) for s in (2, 1, 3)]
    tiles = pl.pallas_call(
        tile_kernel,
        out_shape=sds((ALLOT, 128), BF16),
        in_specs=[VMEM] * 4, out_specs=VMEM, compiler_params=room(8),
        cost_estimate=pl.CostEstimate(flops=4 * USED * 128, bytes_accessed=1_900_000, transcendentals=0),
        name="tiles",
    )(parts[0], r1, r2, r3)
    ig1, ig2, ig3, tiles = lax.optimization_barrier((ig1, ig2, ig3, tiles))
    back = [shifted(ig1, "x", -2), shifted(ig2, "x", -1), shifted(ig3, "x", -3)]
    sums = lax.all_to_all(tiles.reshape(32, 48, 128), ALL, 0, 0, axis_index_groups=groups_second(), tiled=True)
    sums, back[1], back[2] = lax.optimization_barrier((sums, back[1], back[2]))
    s2 = jnp.sum(sums.astype(F32), axis=0)
    at2 = jnp.where(core == 0, lax.axis_index(("z", "yh", "yl")), lax.axis_index(("z", "x")))
    f_hi, f_lo = hi_lo(s2[:ONE] + s2[ONE:2 * ONE])
    special = jnp.concatenate([f_hi, f_lo, jnp.zeros((ONE, 128), BF16)], 0)
    mine = jnp.where(at2 == 4, special, s2.astype(BF16))
    copies = jnp.broadcast_to(mine, (32, 48, 128))
    turned = [group[::-1] for group in groups_second()]
    a1 = lax.all_to_all(copies, ALL, 0, 0, axis_index_groups=turned, tiled=True)
    a1, back = lax.optimization_barrier((a1, back))
    image_grad = ig0 + back[0].astype(F32) + back[1].astype(F32) + back[2].astype(F32)

    b0 = a1.reshape(ALLOT, 128)[:USED]
    b2, b1, b3 = [lax.ppermute(b0, ALL, around(s)) for s in (2, 1, 3)]
    own_half = (b0, b1, b2, b3)
    other_half = [shifted(b, "core", 1) for b in own_half]
    weight_grad, bias_grad, loss = pl.pallas_call(
        last_kernel,
        out_shape=(sds((D, D), F32), sds((D,), F32), sds((1,), F32)),
        in_specs=[SMEM, SMEM] + [VMEM] * 8, out_specs=(ANY, VMEM, SMEM), compiler_params=room(14),
        scratch_shapes=[
            pltpu.VMEM((2, 4, PART, 512), F32), pltpu.VMEM((2, 4, HALF, 128), F32), pltpu.SemaphoreType.DMA((16,)),
        ],
        cost_estimate=pl.CostEstimate(flops=4 * D * D, bytes_accessed=8_500_000, transcendentals=0),
        name="last",
    )(idx, clip_norm, *own_half, *other_half)
    return image_grad, weight_grad, bias_grad, loss


def solution(mesh):
    fine = Mesh(mesh.devices.reshape(NX, NYH, NC, NZ, NYL), ALL)
    placed = (P(ALL, None), P(ALL, None), P(), P(), P(), P(), P(), P())
    return jax.shard_map(
        local, mesh=fine, in_specs=placed, out_specs=(P(ALL, None), P(), P(), P()), check_vma=False
    )
```

```python
import jax
import jax.numpy as jnp
from jax import lax
from jax.experimental import pallas as pl
from jax.experimental.pallas import tpu as pltpu
from jax.sharding import Mesh, PartitionSpec as P

EPS = 1e-06
ALL = ("x", "yh", "core", "z", "yl")
NX, NYH, NC, NZ, NYL = 4, 2, 2, 8, 2
F32, BF16 = jnp.float32, jnp.bfloat16
D, OWN = 1152, 128
WIDE = 640
PART = 288
ONE = 16
LANES = 4
HALF = PART // 2
REAL = 81
USED = 83 * ONE
ALLOT = 96 * ONE
TOTAL = 32768


def room(mib):
    return pltpu.CompilerParams(vmem_limit_bytes=mib * 2**20)


VMEM = pl.BlockSpec(memory_space=pltpu.VMEM)
SMEM = pl.BlockSpec(memory_space=pltpu.SMEM)
ANY = pl.BlockSpec(memory_space=pl.ANY)


def place(x, yh, core, z, yl):
    return (((x * NYH + yh) * NC + core) * NZ + z) * NYL + yl


def every():
    return [
        (x, yh, core, z, yl)
        for x in range(NX) for yh in range(NYH) for core in range(NC) for z in range(NZ) for yl in range(NYL)
    ]


def groups_second():
    out = []
    for x in range(NX):
        out.append([place(x, yh, 0, z, yl) for z in range(NZ) for yh in range(NYH) for yl in range(NYL)])
    for yh in range(NYH):
        for yl in range(NYL):
            out.append([place(x, yh, 1, z, yl) for z in range(NZ) for x in range(NX)])
    return out


def around(distance):
    route = []
    for x, yh, core, z, yl in every():
        if core == 0:
            to = place((x + distance) % NX, yh, core, z, yl)
        else:
            y = (2 * yh + yl + distance) % 4
            to = place(x, y // 2, core, z, y % 2)
        route.append((place(x, yh, core, z, yl), to))
    return route


def spot():
    core = lax.axis_index("core")
    x, y = lax.axis_index("x"), 2 * lax.axis_index("yh") + lax.axis_index("yl")
    return core, jnp.where(core == 0, x, y), jnp.where(core == 0, y, x)


def shifted(block, axis, distance):
    size = lax.axis_size(axis)
    return lax.ppermute(block, axis, [(i, (i + distance) % size) for i in range(size)])


def hi_lo(value):
    hi = value.astype(BF16)
    return hi, (value - hi.astype(F32)).astype(BF16)


def text_kernel(t_ref, w_ref, b_ref, y_ref, inv_ref, flip_ref):
    flip_ref[...] = t_ref[...].T
    u = jnp.dot(t_ref[...], w_ref[...], preferred_element_type=F32) + b_ref[...]
    inv = lax.rsqrt(jnp.sum(u * u, axis=1, keepdims=True) + EPS)
    y_ref[...] = u * inv
    inv_ref[...] = jnp.broadcast_to(inv, (OWN, 128))


def pair_kernel(core_ref, scal_ref, i0, i1, i2, i3, y0, y1, y2, y3, v0, v1, v2, v3,
                gs, keep_ref, give_ref, xb, yb, ext):
    scale, shift, gfac = scal_ref[0], scal_ref[1], scal_ref[2]
    for k, ref in enumerate((i0, i1, i2, i3)):
        rows = slice(k * OWN, (k + 1) * OWN)
        full = ref[...].astype(F32)
        inv = lax.rsqrt(jnp.sum(full * full, axis=1, keepdims=True) + EPS)
        xb[rows, :] = (full * inv).astype(BF16)
        yb[rows, :] = (y0, y1, y2, y3)[k][...].astype(BF16)
    loss = jnp.zeros((1, 1), F32)
    for h in range(2):
        rows = slice(h * 256, (h + 1) * 256)
        z = scale * lax.dot_general(
            xb[rows, :], yb[...], (((1,), (1,)), ((), ())), preferred_element_type=F32
        ) + shift
        if h == 0:
            r = lax.broadcasted_iota(jnp.int32, z.shape, 0)
            c = lax.broadcasted_iota(jnp.int32, z.shape, 1)
            same = (r == c) & (r < OWN)
            signs = jnp.where(same, F32(1.0), F32(-1.0))
            v = -signs * z
        else:
            signs = F32(-1.0)
            v = z
        e = jnp.exp(-jnp.abs(v))
        small = e * (1.0 - e * (0.5 - e * F32(1.0 / 3.0)))
        soft = jnp.maximum(v, 0.0) + jnp.where(e < 0.004, small, jnp.log(1.0 + e))
        loss = loss + jnp.sum(jnp.sum(soft, axis=0, keepdims=True), axis=1, keepdims=True)
        part = 1.0 / (1.0 + e)
        gs[rows, :] = (gfac * signs * jnp.where(v >= 0, part, e * part)).astype(BF16)
    bias = jnp.zeros((1, D), F32)
    first = core_ref[0] == 0
    for h in range(2):
        rows = slice(h * 256, (h + 1) * 256)
        dy = scale * lax.dot_general(
            gs[:, rows], xb[...], (((0,), (0,)), ((), ())), preferred_element_type=F32
        )
        for j in range(2):
            k = 2 * h + j
            here = slice(k * OWN, (k + 1) * OWN)
            dyk = dy[j * OWN:(j + 1) * OWN]
            y = (y0, y1, y2, y3)[k][...]
            du = (dyk - y * jnp.sum(y * dyk, axis=1, keepdims=True)) * (v0, v1, v2, v3)[k][:, 0:1]
            bias = bias + jnp.sum(du, axis=0, keepdims=True)
            parts = [du[:, 512 * c:512 * (c + 1)].astype(BF16) for c in range(2)]
            shared = du[:, 1024:].astype(BF16)
            keep_ref[here, 512:] = shared
            give_ref[here, 512:] = shared

            @pl.when(first)
            def _():
                keep_ref[here, :512] = parts[0]
                give_ref[here, :512] = parts[1]

            @pl.when(jnp.logical_not(first))
            def _():
                give_ref[here, :512] = parts[0]
                keep_ref[here, :512] = parts[1]
    ext[...] = jnp.zeros((ONE, 128), F32)
    for r in range(D // 128):
        ext[r:r + 1, :] = bias[:, r * 128:(r + 1) * 128]
    lane = lax.broadcasted_iota(jnp.int32, (1, 128), 1)
    ext[D // 128:D // 128 + 1, :] = jnp.where(lane == 0, loss, 0.0)
    hi, lo = hi_lo(ext[...])
    for ref in (keep_ref, give_ref):
        ref[4 * OWN:, 128:] = jnp.zeros((2 * ONE, WIDE - 128), BF16)
        ref[4 * OWN:4 * OWN + ONE, :128] = hi
        ref[4 * OWN + ONE:, :128] = lo


def image_kernel(scal_ref, i0, i1, i2, i3, y0, y1, y2, y3, gs, g0, g1, g2, g3, yb):
    scale = scal_ref[0]
    for k, ref in enumerate((y0, y1, y2, y3)):
        yb[k * OWN:(k + 1) * OWN, :] = ref[...].astype(BF16)
    for h in range(2):
        dx2 = scale * jnp.dot(gs[h * 256:(h + 1) * 256, :], yb[...], preferred_element_type=F32)
        for j in range(2):
            k = 2 * h + j
            dx = dx2[j * OWN:(j + 1) * OWN]
            full = (i0, i1, i2, i3)[k][...].astype(F32)
            inv = lax.rsqrt(jnp.sum(full * full, axis=1, keepdims=True) + EPS)
            full = full * inv
            out = (dx - full * jnp.sum(full * dx, axis=1, keepdims=True)) * inv
            target = (g0, g1, g2, g3)[k]
            target[...] = out.astype(target.dtype)


def head_kernel(f0, f1, f2, f3, keep_ref, got_ref, o0, o1, o2, o3, flips, both, rw, shared):
    core, at, _ = spot()
    for k, ref in enumerate((f0, f1, f2, f3)):
        rows, swap = slice(k * OWN, (k + 1) * OWN), slice((k ^ 1) * OWN, ((k ^ 1) + 1) * OWN)
        flips[:, rows] = ref[...]
        both[rows, :] = (keep_ref[rows, :].astype(F32) + got_ref[swap, :].astype(F32)).astype(BF16)
    e = keep_ref[4 * OWN:, :128].astype(F32) + got_ref[4 * OWN:, :128].astype(F32)
    hi, lo = hi_lo(e[:ONE] + e[ONE:])
    for q in range(4):
        part = jnp.dot(flips[q * PART:(q + 1) * PART, :], both[...], preferred_element_type=F32).astype(BF16)
        for t in range(PART // ONE):
            for l in range(LANES):
                n = t * LANES + l
                rw[q, n * ONE:(n + 1) * ONE, :] = part[t * ONE:(t + 1) * ONE, l * 128:(l + 1) * 128]
        shared[q] = part[:, 512:]
        rw[q, 72 * ONE:REAL * ONE, :] = shared[q, pl.ds(pl.multiple_of(core * HALF, HALF), HALF), :]
        rw[q, REAL * ONE:, :] = jnp.zeros((2 * ONE, 128), BF16)
    rw[0, REAL * ONE:(REAL + 1) * ONE, :] = hi
    rw[0, (REAL + 1) * ONE:, :] = lo
    for s, ref in enumerate((o0, o1, o2, o3)):
        ref[...] = rw[lax.rem(at + s, 4)]


def tile_kernel(a0, a1, a2, a3, out):
    total = a0[...].astype(F32) + a1[...].astype(F32) + a2[...].astype(F32) + a3[...].astype(F32)
    group = 3 * ONE
    for j in range(27):
        out[(31 - j) * group:(32 - j) * group, :] = total[j * group:(j + 1) * group].astype(BF16)
    hi, lo = hi_lo(total[REAL * ONE:(REAL + 1) * ONE] + total[(REAL + 1) * ONE:])
    out[4 * group:4 * group + ONE, :] = hi
    out[4 * group + ONE:4 * group + 2 * ONE, :] = lo
    out[4 * group + 2 * ONE:5 * group, :] = jnp.zeros((ONE, 128), BF16)
    out[:4 * group, :] = jnp.zeros((4 * group, 128), BF16)


def copy_kernel(sums_ref, out):
    total = jnp.sum(sums_ref[...].astype(F32), axis=0)
    core, _, _ = spot()
    z = lax.axis_index("z")
    place_in = jnp.where(core == 0, 4 * z + 2 * lax.axis_index("yh") + lax.axis_index("yl"), 4 * z + lax.axis_index("x"))
    hi, lo = hi_lo(total[:ONE] + total[ONE:2 * ONE])
    plain = total.astype(BF16)
    for k in range(32):
        out[k] = plain

    @pl.when(place_in == 4)
    def _():
        for k in range(32):
            out[k, :ONE, :] = hi
            out[k, ONE:2 * ONE, :] = lo


def last_kernel(clip_ref, p0, p1, p2, p3, q0, q1, q2, q3, w_ref, b_ref, loss_ref, slots, shared, out_sem):
    parts = (p0, p1, p2, p3, q0, q1, q2, q3)
    core, at_here, at_there = spot()

    def whole(left, right, at_left, at_right):
        total = jnp.zeros((3 * ONE, 128), F32)
        extra = jnp.zeros((ONE, 128), F32)
        for s in range(4):
            for n in (left + s, right + s):
                def add(t, acc, n=n):
                    v = parts[n][pl.ds(pl.multiple_of(t * 3 * ONE, ONE), 3 * ONE), :].astype(F32)
                    return acc + v * v
                total = lax.fori_loop(0, REAL // 3, add, total, unroll=9)
            here = (lax.rem(at_left + 4 - s, 4) == 0).astype(F32)
            pair = parts[left + s][REAL * ONE:, :].astype(F32)
            extra = extra + here * (pair[:ONE] + pair[ONE:])
        bias = extra[:D // 128]
        square = jnp.sum(total, keepdims=True) + jnp.sum(bias * bias, keepdims=True)
        factor = jnp.minimum(F32(1.0), clip_ref[0] / jnp.sqrt(square))
        outs = []
        for s in range(4):
            for side, n, at in ((0, left + s, at_left), (1, right + s, at_right)):
                def put(t, carry, n=n, side=side, s=s):
                    v = parts[n][pl.ds(pl.multiple_of(t * LANES * ONE, ONE), LANES * ONE), :].astype(F32) * factor
                    rows = pl.ds(pl.multiple_of(t * ONE, ONE), ONE)
                    for l in range(LANES):
                        slots[side, s, rows, l * 128:(l + 1) * 128] = v[l * ONE:(l + 1) * ONE]
                    return carry
                lax.fori_loop(0, PART // ONE, put, 0, unroll=6)
                shared[side, s] = parts[n][72 * ONE:REAL * ONE, :].astype(F32) * factor
                row0 = lax.rem(at + 4 - s, 4) * PART
                whole_rows = pl.ds(pl.multiple_of(row0, PART), PART)
                half_rows = pl.ds(pl.multiple_of(row0 + side * HALF, HALF), HALF)
                for source, target in (
                    (slots.at[side, s], w_ref.at[whole_rows, side * 512:(side + 1) * 512]),
                    (shared.at[side, s], w_ref.at[half_rows, 1024:D]),
                ):
                    out = pltpu.make_async_copy(source, target, out_sem.at[len(outs)])
                    out.start()
                    outs.append(out)
        for r in range(D // 128):
            b_ref[r * 128:(r + 1) * 128] = (bias[r:r + 1] * factor).reshape(128)
        loss_ref[0] = jnp.sum(extra[D // 128:D // 128 + 1, :]) * F32(1.0 / TOTAL)
        for out in outs:
            out.wait()

    @pl.when(core == 0)
    def _():
        whole(0, 4, at_here, at_there)

    @pl.when(core == 1)
    def _():
        whole(4, 0, at_there, at_here)


def sds(shape, kind):
    return jax.ShapeDtypeStruct(shape, kind)


def local(images, texts, head_weight, head_bias, logit_scale, logit_shift, loss_scale, clip_norm):
    core, at, at_other = spot()
    idx = jnp.stack([core, at, at_other]).astype(jnp.int32)
    scal = jnp.stack([logit_scale[0], logit_shift[0], -loss_scale[0] / TOTAL])

    cross = lax.ppermute(texts, ("yh", "core"), [(0, 3), (1, 2), (2, 1), (3, 0)])
    near, cross = lax.optimization_barrier((texts, cross))
    txt = [texts, shifted(near, "core", 1), shifted(texts, "yh", 1), cross]
    img = [images] + [shifted(images, "x", s) for s in (2, 1, 3)]

    bias_row = head_bias[None]
    sides = [
        pl.pallas_call(
            text_kernel,
            out_shape=(sds((OWN, D), F32), sds((OWN, 128), F32), sds((D, OWN), BF16)),
            in_specs=[VMEM] * 3, out_specs=(VMEM,) * 3, compiler_params=room(10),
            cost_estimate=pl.CostEstimate(flops=2 * OWN * D * D, bytes_accessed=3_600_000, transcendentals=OWN),
            name="text_side",
        )(block, head_weight, bias_row)
        for block in txt
    ]
    ys, invs, flips = zip(*sides)
    gs, keep, give = pl.pallas_call(
        pair_kernel,
        out_shape=(sds((4 * OWN, 4 * OWN), BF16),) + (sds((4 * OWN + 2 * ONE, WIDE), BF16),) * 2,
        in_specs=[SMEM, SMEM] + [VMEM] * 12, out_specs=(VMEM,) * 3, compiler_params=room(20),
        scratch_shapes=[
            pltpu.VMEM((4 * OWN, D), BF16), pltpu.VMEM((4 * OWN, D), BF16), pltpu.VMEM((ONE, 128), F32),
        ],
        cost_estimate=pl.CostEstimate(flops=4 * 512 * 512 * D, bytes_accessed=5_500_000, transcendentals=800_000),
        name="pairs",
    )(idx, scal, *img, *ys, *invs)
    ig0, ig1, ig2, ig3 = pl.pallas_call(
        image_kernel,
        out_shape=(sds((OWN, D), F32),) + (sds((OWN, D), BF16),) * 3,
        in_specs=[SMEM] + [VMEM] * 9, out_specs=(VMEM,) * 4, compiler_params=room(20),
        scratch_shapes=[pltpu.VMEM((4 * OWN, D), BF16)],
        cost_estimate=pl.CostEstimate(flops=2 * 512 * 512 * D, bytes_accessed=5_500_000, transcendentals=512),
        name="image_side",
    )(scal, *img, *ys, gs)

    got = shifted(give, "core", 1)
    parts = pl.pallas_call(
        head_kernel,
        out_shape=(sds((USED, 128), BF16),) * 4,
        in_specs=[VMEM] * 6, out_specs=(VMEM,) * 4, compiler_params=room(14),
        scratch_shapes=[
            pltpu.VMEM((D, 4 * OWN), BF16), pltpu.VMEM((4 * OWN, WIDE), BF16),
            pltpu.VMEM((4, USED, 128), BF16), pltpu.VMEM((4, PART, 128), BF16),
        ],
        cost_estimate=pl.CostEstimate(flops=2 * 512 * D * WIDE, bytes_accessed=4_000_000, transcendentals=0),
        name="head",
    )(*flips, keep, got)
    r2, r1, r3 = [lax.ppermute(parts[s], ALL, around(s)) for s in (2, 1, 3)]
    tiles = pl.pallas_call(
        tile_kernel,
        out_shape=sds((ALLOT, 128), BF16),
        in_specs=[VMEM] * 4, out_specs=VMEM, compiler_params=room(8),
        cost_estimate=pl.CostEstimate(flops=4 * USED * 128, bytes_accessed=1_900_000, transcendentals=0),
        name="tiles",
    )(parts[0], r1, r2, r3)
    ig1, ig2, ig3, tiles = lax.optimization_barrier((ig1, ig2, ig3, tiles))
    back = [shifted(ig1, "x", -2), shifted(ig2, "x", -1), shifted(ig3, "x", -3)]
    sums = lax.all_to_all(tiles.reshape(32, 48, 128), ALL, 0, 0, axis_index_groups=groups_second(), tiled=True)
    sums, back[1], back[2] = lax.optimization_barrier((sums, back[1], back[2]))
    copies = pl.pallas_call(
        copy_kernel,
        out_shape=sds((32, 48, 128), BF16),
        in_specs=[VMEM], out_specs=VMEM, compiler_params=room(4),
        cost_estimate=pl.CostEstimate(flops=32 * 48 * 128, bytes_accessed=800_000, transcendentals=0),
        name="copies",
    )(sums)
    turned = [group[::-1] for group in groups_second()]
    a1 = lax.all_to_all(copies, ALL, 0, 0, axis_index_groups=turned, tiled=True)
    a1, back = lax.optimization_barrier((a1, back))
    image_grad = ig0 + back[0].astype(F32) + back[1].astype(F32) + back[2].astype(F32)

    b0 = a1.reshape(ALLOT, 128)[:USED]
    b2, b1, b3 = [lax.ppermute(b0, ALL, around(s)) for s in (2, 1, 3)]
    own_half = (b0, b1, b2, b3)
    other_half = [shifted(b, "core", 1) for b in own_half]
    weight_grad, bias_grad, loss = pl.pallas_call(
        last_kernel,
        out_shape=(sds((D, D), F32), sds((D,), F32), sds((1,), F32)),
        in_specs=[SMEM] + [VMEM] * 8, out_specs=(ANY, VMEM, SMEM), compiler_params=room(14),
        scratch_shapes=[
            pltpu.VMEM((2, 4, PART, 512), F32), pltpu.VMEM((2, 4, HALF, 128), F32), pltpu.SemaphoreType.DMA((16,)),
        ],
        cost_estimate=pl.CostEstimate(flops=4 * D * D, bytes_accessed=8_500_000, transcendentals=0),
        name="last",
    )(clip_norm, *own_half, *other_half)
    return image_grad, weight_grad, bias_grad, loss


def solution(mesh):
    fine = Mesh(mesh.devices.reshape(NX, NYH, NC, NZ, NYL), ALL)
    placed = (P(ALL, None), P(ALL, None), P(), P(), P(), P(), P(), P())
    return jax.shard_map(
        local, mesh=fine, in_specs=placed, out_specs=(P(ALL, None), P(), P(), P()), check_vma=False
    )
```

```python
import jax
import jax.numpy as jnp
from jax import lax
from jax.experimental import pallas as pl
from jax.experimental.pallas import tpu as pltpu
from jax.sharding import Mesh, PartitionSpec as P

EPS = 1e-06
ALL = ("x", "yh", "core", "z", "yl")
NX, NYH, NC, NZ, NYL = 4, 2, 2, 8, 2
F32, BF16 = jnp.float32, jnp.bfloat16
D, OWN = 1152, 128
WIDE = 640
PART = 288
ONE = 16
LANES = 4
HALF = PART // 2
REAL = 81
USED = 83 * ONE
ALLOT = 96 * ONE
TOTAL = 32768


def room(mib):
    return pltpu.CompilerParams(vmem_limit_bytes=mib * 2**20)


VMEM = pl.BlockSpec(memory_space=pltpu.VMEM)
SMEM = pl.BlockSpec(memory_space=pltpu.SMEM)
ANY = pl.BlockSpec(memory_space=pl.ANY)


def place(x, yh, core, z, yl):
    return (((x * NYH + yh) * NC + core) * NZ + z) * NYL + yl


def every():
    return [
        (x, yh, core, z, yl)
        for x in range(NX) for yh in range(NYH) for core in range(NC) for z in range(NZ) for yl in range(NYL)
    ]


def groups_second():
    out = []
    for x in range(NX):
        out.append([place(x, yh, 0, z, yl) for z in range(NZ) for yh in range(NYH) for yl in range(NYL)])
    for yh in range(NYH):
        for yl in range(NYL):
            out.append([place(x, yh, 1, z, yl) for z in range(NZ) for x in range(NX)])
    return out


def around(distance):
    route = []
    for x, yh, core, z, yl in every():
        if core == 0:
            to = place((x + distance) % NX, yh, core, z, yl)
        else:
            y = (2 * yh + yl + distance) % 4
            to = place(x, y // 2, core, z, y % 2)
        route.append((place(x, yh, core, z, yl), to))
    return route


def spot():
    core = lax.axis_index("core")
    x, y = lax.axis_index("x"), 2 * lax.axis_index("yh") + lax.axis_index("yl")
    return core, jnp.where(core == 0, x, y), jnp.where(core == 0, y, x)


def shifted(block, axis, distance):
    size = lax.axis_size(axis)
    return lax.ppermute(block, axis, [(i, (i + distance) % size) for i in range(size)])


def hi_lo(value):
    hi = value.astype(BF16)
    return hi, (value - hi.astype(F32)).astype(BF16)


def text_kernel(t_ref, w_ref, b_ref, y_ref, inv_ref, flip_ref):
    flip_ref[...] = t_ref[...].T
    u = jnp.dot(t_ref[...], w_ref[...], preferred_element_type=F32) + b_ref[...]
    inv = lax.rsqrt(jnp.sum(u * u, axis=1, keepdims=True) + EPS)
    y_ref[...] = u * inv
    inv_ref[...] = jnp.broadcast_to(inv, (OWN, 128))


def pair_kernel(scal_ref, i0, i1, i2, i3, y0, y1, y2, y3, v0, v1, v2, v3,
                gs, keep_ref, give_ref, xb, yb, ext):
    scale, shift, gfac = scal_ref[0], scal_ref[1], scal_ref[2]
    for k, ref in enumerate((i0, i1, i2, i3)):
        rows = slice(k * OWN, (k + 1) * OWN)
        full = ref[...].astype(F32)
        inv = lax.rsqrt(jnp.sum(full * full, axis=1, keepdims=True) + EPS)
        xb[rows, :] = (full * inv).astype(BF16)
        yb[rows, :] = (y0, y1, y2, y3)[k][...].astype(BF16)
    loss = jnp.zeros((1, 1), F32)
    for h in range(2):
        rows = slice(h * 256, (h + 1) * 256)
        z = scale * lax.dot_general(
            xb[rows, :], yb[...], (((1,), (1,)), ((), ())), preferred_element_type=F32
        ) + shift
        if h == 0:
            r = lax.broadcasted_iota(jnp.int32, z.shape, 0)
            c = lax.broadcasted_iota(jnp.int32, z.shape, 1)
            same = (r == c) & (r < OWN)
            signs = jnp.where(same, F32(1.0), F32(-1.0))
            v = -signs * z
        else:
            signs = F32(-1.0)
            v = z
        e = jnp.exp(-jnp.abs(v))
        small = e * (1.0 - e * (0.5 - e * F32(1.0 / 3.0)))
        soft = jnp.maximum(v, 0.0) + jnp.where(e < 0.004, small, jnp.log(1.0 + e))
        loss = loss + jnp.sum(jnp.sum(soft, axis=0, keepdims=True), axis=1, keepdims=True)
        part = 1.0 / (1.0 + e)
        gs[rows, :] = (gfac * signs * jnp.where(v >= 0, part, e * part)).astype(BF16)
    bias = jnp.zeros((1, D), F32)
    first = scal_ref[3] < 0.5
    for h in range(2):
        rows = slice(h * 256, (h + 1) * 256)
        dy = scale * lax.dot_general(
            gs[:, rows], xb[...], (((0,), (0,)), ((), ())), preferred_element_type=F32
        )
        for j in range(2):
            k = 2 * h + j
            here = slice(k * OWN, (k + 1) * OWN)
            dyk = dy[j * OWN:(j + 1) * OWN]
            y = (y0, y1, y2, y3)[k][...]
            du = (dyk - y * jnp.sum(y * dyk, axis=1, keepdims=True)) * (v0, v1, v2, v3)[k][:, 0:1]
            bias = bias + jnp.sum(du, axis=0, keepdims=True)
            parts = [du[:, 512 * c:512 * (c + 1)].astype(BF16) for c in range(2)]
            shared = du[:, 1024:].astype(BF16)
            keep_ref[here, 512:] = shared
            give_ref[here, 512:] = shared

            @pl.when(first)
            def _():
                keep_ref[here, :512] = parts[0]
                give_ref[here, :512] = parts[1]

            @pl.when(jnp.logical_not(first))
            def _():
                give_ref[here, :512] = parts[0]
                keep_ref[here, :512] = parts[1]
    ext[...] = jnp.zeros((ONE, 128), F32)
    for r in range(D // 128):
        ext[r:r + 1, :] = bias[:, r * 128:(r + 1) * 128]
    lane = lax.broadcasted_iota(jnp.int32, (1, 128), 1)
    ext[D // 128:D // 128 + 1, :] = jnp.where(lane == 0, loss, 0.0)
    hi, lo = hi_lo(ext[...])
    for ref in (keep_ref, give_ref):
        ref[4 * OWN:, 128:] = jnp.zeros((2 * ONE, WIDE - 128), BF16)
        ref[4 * OWN:4 * OWN + ONE, :128] = hi
        ref[4 * OWN + ONE:, :128] = lo


def image_kernel(scal_ref, i0, i1, i2, i3, y0, y1, y2, y3, gs, g0, g1, g2, g3, yb):
    scale = scal_ref[0]
    for k, ref in enumerate((y0, y1, y2, y3)):
        yb[k * OWN:(k + 1) * OWN, :] = ref[...].astype(BF16)
    for h in range(2):
        dx2 = scale * jnp.dot(gs[h * 256:(h + 1) * 256, :], yb[...], preferred_element_type=F32)
        for j in range(2):
            k = 2 * h + j
            dx = dx2[j * OWN:(j + 1) * OWN]
            full = (i0, i1, i2, i3)[k][...].astype(F32)
            inv = lax.rsqrt(jnp.sum(full * full, axis=1, keepdims=True) + EPS)
            full = full * inv
            out = (dx - full * jnp.sum(full * dx, axis=1, keepdims=True)) * inv
            target = (g0, g1, g2, g3)[k]
            target[...] = out.astype(target.dtype)


def head_kernel(f0, f1, f2, f3, keep_ref, got_ref, o0, o1, o2, o3, flips, both, rw, shared):
    core, at, _ = spot()
    for k, ref in enumerate((f0, f1, f2, f3)):
        rows, swap = slice(k * OWN, (k + 1) * OWN), slice((k ^ 1) * OWN, ((k ^ 1) + 1) * OWN)
        flips[:, rows] = ref[...]
        both[rows, :] = (keep_ref[rows, :].astype(F32) + got_ref[swap, :].astype(F32)).astype(BF16)
    e = keep_ref[4 * OWN:, :128].astype(F32) + got_ref[4 * OWN:, :128].astype(F32)
    hi, lo = hi_lo(e[:ONE] + e[ONE:])
    for q in range(4):
        part = jnp.dot(flips[q * PART:(q + 1) * PART, :], both[...], preferred_element_type=F32).astype(BF16)
        for t in range(PART // ONE):
            for l in range(LANES):
                n = t * LANES + l
                rw[q, n * ONE:(n + 1) * ONE, :] = part[t * ONE:(t + 1) * ONE, l * 128:(l + 1) * 128]
        shared[q] = part[:, 512:]
        rw[q, 72 * ONE:REAL * ONE, :] = shared[q, pl.ds(pl.multiple_of(core * HALF, HALF), HALF), :]
        rw[q, REAL * ONE:, :] = jnp.zeros((2 * ONE, 128), BF16)
    rw[0, REAL * ONE:(REAL + 1) * ONE, :] = hi
    rw[0, (REAL + 1) * ONE:, :] = lo
    for s, ref in enumerate((o0, o1, o2, o3)):
        ref[...] = rw[lax.rem(at + s, 4)]


def tile_kernel(a0, a1, a2, a3, out):
    total = a0[...].astype(F32) + a1[...].astype(F32) + a2[...].astype(F32) + a3[...].astype(F32)
    group = 3 * ONE
    for j in range(27):
        out[(31 - j) * group:(32 - j) * group, :] = total[j * group:(j + 1) * group].astype(BF16)
    hi, lo = hi_lo(total[REAL * ONE:(REAL + 1) * ONE] + total[(REAL + 1) * ONE:])
    out[4 * group:4 * group + ONE, :] = hi
    out[4 * group + ONE:4 * group + 2 * ONE, :] = lo
    out[4 * group + 2 * ONE:5 * group, :] = jnp.zeros((ONE, 128), BF16)
    out[:4 * group, :] = jnp.zeros((4 * group, 128), BF16)


def copy_kernel(sums_ref, out):
    total = jnp.sum(sums_ref[...].astype(F32), axis=0)
    core, _, _ = spot()
    z = lax.axis_index("z")
    place_in = jnp.where(core == 0, 4 * z + 2 * lax.axis_index("yh") + lax.axis_index("yl"), 4 * z + lax.axis_index("x"))
    hi, lo = hi_lo(total[:ONE] + total[ONE:2 * ONE])
    plain = total.astype(BF16)
    for k in range(32):
        out[k] = plain

    @pl.when(place_in == 4)
    def _():
        for k in range(32):
            out[k, :ONE, :] = hi
            out[k, ONE:2 * ONE, :] = lo


def last_kernel(clip_ref, p0, p1, p2, p3, q0, q1, q2, q3, w_ref, b_ref, loss_ref, slots, shared, out_sem):
    parts = (p0, p1, p2, p3, q0, q1, q2, q3)
    core, at_here, at_there = spot()

    def whole(left, right, at_left, at_right):
        total = jnp.zeros((3 * ONE, 128), F32)
        extra = jnp.zeros((ONE, 128), F32)
        for s in range(4):
            for n in (left + s, right + s):
                def add(t, acc, n=n):
                    v = parts[n][pl.ds(pl.multiple_of(t * 3 * ONE, ONE), 3 * ONE), :].astype(F32)
                    return acc + v * v
                total = lax.fori_loop(0, REAL // 3, add, total, unroll=9)
            here = (lax.rem(at_left + 4 - s, 4) == 0).astype(F32)
            pair = parts[left + s][REAL * ONE:, :].astype(F32)
            extra = extra + here * (pair[:ONE] + pair[ONE:])
        bias = extra[:D // 128]
        square = jnp.sum(total, keepdims=True) + jnp.sum(bias * bias, keepdims=True)
        factor = jnp.minimum(F32(1.0), clip_ref[0] / jnp.sqrt(square))
        outs = []
        for s in range(4):
            for side, n, at in ((0, left + s, at_left), (1, right + s, at_right)):
                def put(t, carry, n=n, side=side, s=s):
                    v = parts[n][pl.ds(pl.multiple_of(t * LANES * ONE, ONE), LANES * ONE), :].astype(F32) * factor
                    rows = pl.ds(pl.multiple_of(t * ONE, ONE), ONE)
                    for l in range(LANES):
                        slots[side, s, rows, l * 128:(l + 1) * 128] = v[l * ONE:(l + 1) * ONE]
                    return carry
                lax.fori_loop(0, PART // ONE, put, 0, unroll=6)
                shared[side, s] = parts[n][72 * ONE:REAL * ONE, :].astype(F32) * factor
                row0 = lax.rem(at + 4 - s, 4) * PART
                whole_rows = pl.ds(pl.multiple_of(row0, PART), PART)
                half_rows = pl.ds(pl.multiple_of(row0 + side * HALF, HALF), HALF)
                for source, target in (
                    (slots.at[side, s], w_ref.at[whole_rows, side * 512:(side + 1) * 512]),
                    (shared.at[side, s], w_ref.at[half_rows, 1024:D]),
                ):
                    out = pltpu.make_async_copy(source, target, out_sem.at[len(outs)])
                    out.start()
                    outs.append(out)
        for r in range(D // 128):
            b_ref[r * 128:(r + 1) * 128] = (bias[r:r + 1] * factor).reshape(128)
        loss_ref[0] = jnp.sum(extra[D // 128:D // 128 + 1, :]) * F32(1.0 / TOTAL)
        for out in outs:
            out.wait()

    @pl.when(core == 0)
    def _():
        whole(0, 4, at_here, at_there)

    @pl.when(core == 1)
    def _():
        whole(4, 0, at_there, at_here)


def sds(shape, kind):
    return jax.ShapeDtypeStruct(shape, kind)


def local(images, texts, head_weight, head_bias, logit_scale, logit_shift, loss_scale, clip_norm):
    core, at, at_other = spot()
    spots = jnp.stack([core, at, at_other]).astype(F32)
    scal = jnp.concatenate([jnp.stack([logit_scale[0], logit_shift[0], -loss_scale[0] / TOTAL]), spots])

    cross = lax.ppermute(texts, ("yh", "core"), [(0, 3), (1, 2), (2, 1), (3, 0)])
    near, cross = lax.optimization_barrier((texts, cross))
    txt = [texts, shifted(near, "core", 1), shifted(texts, "yh", 1), cross]
    img = [images] + [shifted(images, "x", s) for s in (2, 1, 3)]

    bias_row = head_bias[None]
    sides = [
        pl.pallas_call(
            text_kernel,
            out_shape=(sds((OWN, D), F32), sds((OWN, 128), F32), sds((D, OWN), BF16)),
            in_specs=[VMEM] * 3, out_specs=(VMEM,) * 3, compiler_params=room(10),
            cost_estimate=pl.CostEstimate(flops=2 * OWN * D * D, bytes_accessed=3_600_000, transcendentals=OWN),
            name="text_side",
        )(block, head_weight, bias_row)
        for block in txt
    ]
    ys, invs, flips = zip(*sides)
    gs, keep, give = pl.pallas_call(
        pair_kernel,
        out_shape=(sds((4 * OWN, 4 * OWN), BF16),) + (sds((4 * OWN + 2 * ONE, WIDE), BF16),) * 2,
        in_specs=[SMEM] + [VMEM] * 12, out_specs=(VMEM,) * 3, compiler_params=room(20),
        scratch_shapes=[
            pltpu.VMEM((4 * OWN, D), BF16), pltpu.VMEM((4 * OWN, D), BF16), pltpu.VMEM((ONE, 128), F32),
        ],
        cost_estimate=pl.CostEstimate(flops=4 * 512 * 512 * D, bytes_accessed=5_500_000, transcendentals=800_000),
        name="pairs",
    )(scal, *img, *ys, *invs)
    ig0, ig1, ig2, ig3 = pl.pallas_call(
        image_kernel,
        out_shape=(sds((OWN, D), F32),) + (sds((OWN, D), BF16),) * 3,
        in_specs=[SMEM] + [VMEM] * 9, out_specs=(VMEM,) * 4, compiler_params=room(20),
        scratch_shapes=[pltpu.VMEM((4 * OWN, D), BF16)],
        cost_estimate=pl.CostEstimate(flops=2 * 512 * 512 * D, bytes_accessed=5_500_000, transcendentals=512),
        name="image_side",
    )(scal, *img, *ys, gs)

    got = shifted(give, "core", 1)
    parts = pl.pallas_call(
        head_kernel,
        out_shape=(sds((USED, 128), BF16),) * 4,
        in_specs=[VMEM] * 6, out_specs=(VMEM,) * 4, compiler_params=room(14),
        scratch_shapes=[
            pltpu.VMEM((D, 4 * OWN), BF16), pltpu.VMEM((4 * OWN, WIDE), BF16),
            pltpu.VMEM((4, USED, 128), BF16), pltpu.VMEM((4, PART, 128), BF16),
        ],
        cost_estimate=pl.CostEstimate(flops=2 * 512 * D * WIDE, bytes_accessed=4_000_000, transcendentals=0),
        name="head",
    )(*flips, keep, got)
    r2, r1, r3 = [lax.ppermute(parts[s], ALL, around(s)) for s in (2, 1, 3)]
    tiles = pl.pallas_call(
        tile_kernel,
        out_shape=sds((ALLOT, 128), BF16),
        in_specs=[VMEM] * 4, out_specs=VMEM, compiler_params=room(8),
        cost_estimate=pl.CostEstimate(flops=4 * USED * 128, bytes_accessed=1_900_000, transcendentals=0),
        name="tiles",
    )(parts[0], r1, r2, r3)
    ig1, ig2, ig3, tiles = lax.optimization_barrier((ig1, ig2, ig3, tiles))
    back = [shifted(ig1, "x", -2), shifted(ig2, "x", -1), shifted(ig3, "x", -3)]
    sums = lax.all_to_all(tiles.reshape(32, 48, 128), ALL, 0, 0, axis_index_groups=groups_second(), tiled=True)
    sums, back[1], back[2] = lax.optimization_barrier((sums, back[1], back[2]))
    copies = pl.pallas_call(
        copy_kernel,
        out_shape=sds((32, 48, 128), BF16),
        in_specs=[VMEM], out_specs=VMEM, compiler_params=room(4),
        cost_estimate=pl.CostEstimate(flops=32 * 48 * 128, bytes_accessed=800_000, transcendentals=0),
        name="copies",
    )(sums)
    turned = [group[::-1] for group in groups_second()]
    a1 = lax.all_to_all(copies, ALL, 0, 0, axis_index_groups=turned, tiled=True)
    a1, back = lax.optimization_barrier((a1, back))
    image_grad = ig0 + back[0].astype(F32) + back[1].astype(F32) + back[2].astype(F32)

    b0 = a1.reshape(ALLOT, 128)[:USED]
    b2, b1, b3 = [lax.ppermute(b0, ALL, around(s)) for s in (2, 1, 3)]
    own_half = (b0, b1, b2, b3)
    other_half = [shifted(b, "core", 1) for b in own_half]
    weight_grad, bias_grad, loss = pl.pallas_call(
        last_kernel,
        out_shape=(sds((D, D), F32), sds((D,), F32), sds((1,), F32)),
        in_specs=[SMEM] + [VMEM] * 8, out_specs=(ANY, VMEM, SMEM), compiler_params=room(14),
        scratch_shapes=[
            pltpu.VMEM((2, 4, PART, 512), F32), pltpu.VMEM((2, 4, HALF, 128), F32), pltpu.SemaphoreType.DMA((16,)),
        ],
        cost_estimate=pl.CostEstimate(flops=4 * D * D, bytes_accessed=8_500_000, transcendentals=0),
        name="last",
    )(clip_norm, *own_half, *other_half)
    return image_grad, weight_grad, bias_grad, loss


def solution(mesh):
    fine = Mesh(mesh.devices.reshape(NX, NYH, NC, NZ, NYL), ALL)
    placed = (P(ALL, None), P(ALL, None), P(), P(), P(), P(), P(), P())
    return jax.shard_map(
        local, mesh=fine, in_specs=placed, out_specs=(P(ALL, None), P(), P(), P()), check_vma=False
    )
```
